32 devices in a mesh: groups: 2 (over y), shard: 4 (over z), dp: 4 (over x, core).
Axes of the slice: x: 2, y: 2, z: 4, core: 2. Of those that a mesh axis runs over, the one named last changes fastest.
Arguments:
- maps_in: bfloat16 [32, 32, 1536], P(('groups', 'dp')), parts along dimension 0, may hold values from -6 to 6
- filters: bfloat16 [49, 1536], replicated, may hold values from -2 to 2
- w_expand: bfloat16 [1536, 6144], P(None, 'shard'), may hold values from -0.15625 to 0.15625
- w_project: bfloat16 [6144, 1536], P('shard'), may hold values from -0.078125 to 0.078125
- cotangent: bfloat16 [32, 32, 1536], P(('groups', 'dp')), parts along dimension 0, may hold values from -6 to 6
Outputs:
- block_out: bfloat16 [32, 32, 1536], P(('groups', 'dp')), parts along dimension 0
- grad_input: bfloat16 [32, 32, 1536], P(('groups', 'dp')), parts along dimension 0
- grad_expand: float32 [3072, 6144], P(('groups', 'dp'), 'shard'), parts along dimension 0
- grad_project: float32 [12288, 1536], P(('groups', 'shard'), 'dp'), parts along dimension 0
- grad_filters: float32 [98, 1536], P('groups'), parts along dimension 0
The draws below stay inside these ranges and needn't reach their ends.
There are 2 independent parts, one for each index of `groups`. The reference program is written for one: setup_inputs(seed, part) draws one part's arguments, and reference() takes and returns one part's arrays. A program takes and returns all parts, laid end to end along the dimension named above; an argument that names none is the same for every part. Nothing has to cross between parts.
All inputs are finite; a program needn't handle non-finite values.
Results may differ from the reference program's by a relative error of at most 0.015.
Values may be sent and summed in bfloat16 or wider, within the bound.
A program may use at most 128 MiB of HBM per device.

```python
import math
import jax
import jax.numpy as jnp
from jax import lax

C = 1536
HID = 6144
KS = 7
MAP_COLS = 32
MAP_ROWS = 16
N_SHARD = 4


def draw_filters(key, part):
    noise_key = jax.random.fold_in(key, 11)
    scale_key = jax.random.fold_in(key, 23)
    base = jnp.clip(jax.random.normal(noise_key, (KS * KS, C), jnp.float32), -4.0, 4.0)
    scales = jnp.exp(jax.random.uniform(scale_key, (1, C), jnp.float32, math.log(0.3), math.log(3.0)))
    return (base * scales / KS).astype(jnp.bfloat16)


def block_scale(own_key, dims, pieces, least, top_value):
    def one(dim, blocks):
        steps = jax.random.uniform(jax.random.fold_in(jax.random.fold_in(own_key, 6), dim), (blocks,), jnp.float32, least / len(pieces), top_value / len(pieces))
        return jnp.repeat(jnp.exp(steps), dims[dim] // blocks).reshape((-1,) + (1,) * (len(dims) - dim - 1))

    level = one(*pieces[0])
    for cut in pieces[1:]:
        level = level * one(*cut)
    return level


def bell_draw(stream_key, extent, deviation, limit, cuts=(), kind=jnp.bfloat16):
    entries = jax.random.normal(stream_key, extent, jnp.float32) * deviation
    if len(cuts) > 0:
        entries = block_scale(stream_key, extent, cuts, -0.22, 0.18) * entries
    return jnp.clip(entries, min=-limit, max=limit).astype(kind)


def setup_inputs(seed: int = 0, part: int = 0) -> dict:
    keys = jax.random.split(jax.random.key(seed), 6)
    part_keys = jax.random.split(jax.random.fold_in(keys[5], part), 6)
    return {
        "maps_in": bell_draw(part_keys[0], (MAP_ROWS, MAP_COLS, C), 1.0, 6.0, ((0, 4),)),
        "filters": draw_filters(jax.random.fold_in(keys[5], 71), part),
        "w_expand": bell_draw(keys[2], (C, HID), C ** -0.5, 0.15625, ((1, 4),)),
        "w_project": bell_draw(keys[3], (HID, C), HID ** -0.5, 0.078125, ((0, 4),)),
        "cotangent": bell_draw(part_keys[4], (MAP_ROWS, MAP_COLS, C), 1.0, 6.0, ((0, 4),)),
    }


def gelu_parts(hidden):
    cdf = 0.5 * (1.0 + jax.scipy.special.erf(hidden * 0.7071067811865476))
    density = jnp.exp(-0.5 * hidden * hidden) * 0.3989422804014327
    return (hidden * cdf, cdf + hidden * density)

def norm_stats(conv_rows):
    centered = conv_rows - lax.optimization_barrier(jnp.mean(conv_rows, axis=-1, keepdims=True))
    variance = lax.optimization_barrier(jnp.mean(centered * centered, axis=-1, keepdims=True))
    inv_scale = lax.rsqrt(variance + 1e-06)
    return (centered * inv_scale, inv_scale)

def norm_back(d_normed, scaled, inv_scale):
    first = lax.optimization_barrier(jnp.mean(d_normed, axis=-1, keepdims=True))
    second = lax.optimization_barrier(jnp.mean(d_normed * scaled, axis=-1, keepdims=True))
    return inv_scale * (d_normed - first - scaled * second)

def blocked_product(left, right, contract_right):
    width = left.shape[1] // N_SHARD
    out_cols = right.shape[1 - contract_right]

    def add_block(index, total):
        left_block = lax.dynamic_slice_in_dim(left, index * width, width, 1)
        right_block = lax.dynamic_slice_in_dim(right, index * width, width, contract_right)
        if contract_right == 1:
            right_block = right_block.T
        part_sum = jnp.dot(left_block, right_block, precision=lax.Precision.HIGHEST)
        rounded = lax.optimization_barrier(part_sum.astype(jnp.bfloat16))
        return total + rounded.astype(jnp.float32)
    start = jnp.zeros((left.shape[0], out_cols), jnp.float32)
    return lax.fori_loop(0, N_SHARD, add_block, start)

def reference(maps_in, filters, w_expand, w_project, cotangent):
    reach = KS // 2
    taps_f32 = filters.astype(jnp.float32)
    input_f32 = maps_in.astype(jnp.float32)
    padded_in = jnp.pad(input_f32, ((reach, reach), (reach, reach), (0, 0)))
    conv_out = jnp.zeros(input_f32.shape, jnp.float32)
    for tap in range(KS * KS):
        tap_row, tap_col = divmod(tap, KS)
        conv_out = conv_out + padded_in[tap_row:tap_row + MAP_ROWS, tap_col:tap_col + MAP_COLS] * taps_f32[tap]
    scaled, inv_scale = norm_stats(conv_out.reshape(-1, C))
    normed = scaled.astype(jnp.bfloat16).astype(jnp.float32)
    expand_f32 = w_expand.astype(jnp.float32)
    project_f32 = w_project.astype(jnp.float32)
    hidden = jnp.dot(normed, expand_f32, precision=lax.Precision.HIGHEST)
    activ, slope = gelu_parts(hidden)
    act = activ.astype(jnp.bfloat16).astype(jnp.float32)
    proj = blocked_product(act, project_f32, 0)
    block_out = (input_f32.reshape(-1, C) + proj).astype(jnp.bfloat16).reshape(MAP_ROWS, MAP_COLS, C)
    cot_rows = cotangent.reshape(-1, C).astype(jnp.float32)
    d_act = jnp.dot(cot_rows, project_f32.T, precision=lax.Precision.HIGHEST)
    d_hidden = (d_act * slope).astype(jnp.bfloat16).astype(jnp.float32)
    grad_project = jnp.dot(act.T, cot_rows, precision=lax.Precision.HIGHEST)
    grad_expand = jnp.dot(normed.T, d_hidden, precision=lax.Precision.HIGHEST)
    d_normed = blocked_product(d_hidden, expand_f32, 1)
    d_conv = norm_back(d_normed, scaled, inv_scale).astype(jnp.bfloat16).astype(jnp.float32)
    d_conv = d_conv.reshape(MAP_ROWS, MAP_COLS, C)
    padded_grad = jnp.pad(d_conv, ((reach, reach), (reach, reach), (0, 0)))
    back_sum = cotangent.astype(jnp.float32)
    filter_rows = []
    for tap in range(KS * KS):
        tap_row, tap_col = divmod(tap, KS)
        back_sum = back_sum + padded_grad[2 * reach - tap_row:2 * reach - tap_row + MAP_ROWS, 2 * reach - tap_col:2 * reach - tap_col + MAP_COLS] * taps_f32[tap]
        filter_rows.append(lax.optimization_barrier(jnp.sum(d_conv * padded_in[tap_row:tap_row + MAP_ROWS, tap_col:tap_col + MAP_COLS], axis=(0, 1))))
    grad_input = back_sum.astype(jnp.bfloat16)
    grad_filters = jnp.stack(filter_rows, axis=0)
    return (block_out, grad_input, grad_expand, grad_project, grad_filters)
```

```python
import functools

import jax
import jax.numpy as jnp
from jax import lax
from jax.experimental import pallas as pl
from jax.experimental.pallas import tpu as pltpu
from jax.sharding import PartitionSpec as P

KS = 7
REACH = KS // 2
LANE = 128
PAD = 8
F32 = jnp.float32
BF16 = jnp.bfloat16
MESH = pl.DeviceIdType.MESH


def extended(block, sides, width):
    for axis, dim in sides:
        count = lax.axis_size(axis)
        forward = [(i, i + 1) for i in range(count - 1)]
        backward = [(target, source) for source, target in forward]
        low = lax.ppermute(
            lax.slice_in_dim(block, block.shape[dim] - width, None, axis=dim), axis, forward
        )
        high = lax.ppermute(lax.slice_in_dim(block, 0, width, axis=dim), axis, backward)
        block = jnp.concatenate([low, block, high], axis=dim)
    return block


def gelu_parts(hidden):
    cdf = 0.5 * (1.0 + lax.erf(hidden * 0.7071067811865476))
    density = jnp.exp(-0.5 * hidden * hidden) * 0.3989422804014327
    return (hidden * cdf, cdf + hidden * density)


def norm_stats(conv_rows):
    centered = conv_rows - jnp.mean(conv_rows, axis=-1, keepdims=True)
    variance = jnp.mean(centered * centered, axis=-1, keepdims=True)
    inv_scale = lax.rsqrt(variance + 1e-06)
    return (centered * inv_scale, inv_scale)


def norm_back(d_normed, scaled, inv_scale):
    first = jnp.mean(d_normed, axis=-1, keepdims=True)
    second = jnp.mean(d_normed * scaled, axis=-1, keepdims=True)
    return inv_scale * (d_normed - first - scaled * second)


def plain_body(maps_in, filters, w_expand, w_project, cotangent):
    reach = KS // 2
    rows, cols, width = maps_in.shape
    count = rows * cols
    taps_f32 = filters.astype(jnp.float32)
    halo_in = extended(maps_in, (("dp", 0),), reach)
    padded_in = jnp.pad(halo_in, ((0, 0), (reach, reach), (0, 0)))
    conv_out = jnp.zeros((rows, cols, width), jnp.float32)
    for tap in range(KS * KS):
        tap_row, tap_col = divmod(tap, KS)
        conv_out = (
            conv_out
            + padded_in[tap_row : tap_row + rows, tap_col : tap_col + cols].astype(jnp.float32)
            * taps_f32[tap]
        )
    scaled, inv_scale = norm_stats(conv_out.reshape(count, width))
    normed = scaled.astype(jnp.bfloat16)
    hidden = jnp.dot(normed, w_expand, preferred_element_type=jnp.float32)
    activ, slope = gelu_parts(hidden)
    act = activ.astype(jnp.bfloat16)
    partial_out = jnp.dot(act, w_project, preferred_element_type=jnp.float32)
    cot_rows = cotangent.reshape(count, width)
    summed_out = lax.psum(partial_out.astype(jnp.bfloat16), "shard").astype(jnp.float32)
    d_act = lax.dot_general(
        cot_rows, w_project, (((1,), (1,)), ((), ())), preferred_element_type=jnp.float32
    )
    d_hidden = (d_act * slope).astype(jnp.bfloat16)
    grad_proj_local = lax.dot_general(
        act, cot_rows, (((0,), (0,)), ((), ())), preferred_element_type=jnp.float32
    )
    grad_exp_local = lax.dot_general(
        normed, d_hidden, (((0,), (0,)), ((), ())), preferred_element_type=jnp.float32
    )
    partial_norm = lax.dot_general(
        d_hidden, w_expand, (((1,), (1,)), ((), ())), preferred_element_type=jnp.float32
    )
    d_normed = lax.psum(partial_norm.astype(jnp.bfloat16), "shard").astype(jnp.float32)
    d_conv = norm_back(d_normed, scaled, inv_scale).astype(jnp.bfloat16)
    block_out = (
        (maps_in.reshape(count, width).astype(jnp.float32) + summed_out)
        .astype(jnp.bfloat16)
        .reshape(rows, cols, width)
    )
    grad_expand, grad_project = (
        lax.psum_scatter(
            grad_exp_local.astype(jnp.bfloat16), "dp", scatter_dimension=0, tiled=True
        ).astype(jnp.float32),
        lax.psum_scatter(
            grad_proj_local.astype(jnp.bfloat16), "dp", scatter_dimension=1, tiled=True
        ).astype(jnp.float32),
    )
    d_conv = d_conv.reshape(rows, cols, width)
    halo_grad = extended(d_conv, (("dp", 0),), reach)
    padded_grad = jnp.pad(halo_grad, ((0, 0), (reach, reach), (0, 0)))
    conv_grad = d_conv.astype(jnp.float32)
    back_sum = cotangent.astype(jnp.float32)
    filter_rows = []
    for tap in range(KS * KS):
        tap_row, tap_col = divmod(tap, KS)
        back_sum = (
            back_sum
            + padded_grad[
                2 * reach - tap_row : 2 * reach - tap_row + rows,
                2 * reach - tap_col : 2 * reach - tap_col + cols,
            ].astype(jnp.float32)
            * taps_f32[tap]
        )
        filter_rows.append(
            jnp.sum(
                conv_grad
                * padded_in[tap_row : tap_row + rows, tap_col : tap_col + cols].astype(jnp.float32),
                axis=(0, 1),
            )
        )
    grad_input = back_sum.astype(jnp.bfloat16)
    grad_filters = lax.psum(jnp.stack(filter_rows, axis=0).astype(jnp.bfloat16), "dp").astype(
        jnp.float32
    )
    return (block_out, grad_input, grad_expand, grad_project, grad_filters)


CONTRACT_LAST = (((1,), (1,)), ((), ()))
CONTRACT_FIRST = (((0,), (0,)), ((), ()))


def kernel(
    S, R, W, C, H,
    maps_ref, fil_ref, cot_ref, we_hbm, wp_hbm,
    out_hbm, gin_hbm, ge_hbm, gp_hbm, gf_ref,
    we, wp, fil, mp, halo_lo, halo_hi, conv, scaled, invs, dact,
    nrm, cots, act, dh, ns, cs, pn, rn, po, ro, bo, st, rst,
    dcv, dlo, dhi, dpad, fpart, fsum, fall, gi, ge, gp,
    send, recv, loc,
):
    N = R * W
    CH = C // S
    DC = C // 4
    g = lax.axis_index("groups")
    s = lax.axis_index("shard")
    d = lax.axis_index("dp")
    pair_core = d + 1 - 2 * lax.rem(d, 2)
    pair_chip = lax.rem(d + 2, 4)
    peers = [lax.rem(s + k, S) for k in range(S)]
    has_lo = d > 0
    has_hi = d < 3

    def chan(i):
        return pl.ds(pl.multiple_of(i * CH, LANE), CH)

    def dpcols(i):
        return pl.ds(pl.multiple_of(i * DC, LANE), DC)

    counter = [0]

    def remote(src, dst, shard, dp):
        i = counter[0]
        counter[0] += 1
        return pltpu.make_async_remote_copy(
            src_ref=src, dst_ref=dst, send_sem=send.at[i], recv_sem=recv.at[i],
            device_id=(g, shard, dp), device_id_type=MESH,
        )

    def move(src, dst, i):
        return pltpu.make_async_copy(src, dst, loc.at[i])

    cp_wp = move(wp_hbm, wp, 0)
    cp_we = move(we_hbm, we, 1)
    cp_wp.start()
    cp_we.start()

    barrier = pltpu.get_barrier_semaphore()
    for k in range(1, S):
        pl.semaphore_signal(barrier, inc=1, device_id=(g, peers[k], d), device_id_type=MESH)
    for k in range(1, 4):
        pl.semaphore_signal(
            barrier, inc=1, device_id=(g, s, lax.rem(d + k, 4)), device_id_type=MESH
        )
    pl.semaphore_wait(barrier, S - 1 + 3)

    lo_dp = jnp.maximum(d - 1, 0)
    hi_dp = jnp.minimum(d + 1, 3)
    to_hi = remote(maps_ref.at[pl.ds(R - REACH, REACH)], halo_lo, s, hi_dp)
    to_lo = remote(maps_ref.at[pl.ds(0, REACH)], halo_hi, s, lo_dp)

    @pl.when(has_hi)
    def _():
        to_hi.start()

    @pl.when(has_lo)
    def _():
        to_lo.start()

    c_cot = remote(cot_ref, cots, s, pair_chip)
    c_cot.start()

    fil[pl.ds(0, KS * KS), :] = fil_ref[...].astype(F32)
    for r in range(R + 2 * REACH):
        mp[r, pl.ds(0, PAD), :] = jnp.zeros((PAD, C), F32)
        mp[r, pl.ds(PAD + W, PAD), :] = jnp.zeros((PAD, C), F32)
        dpad[r, pl.ds(0, PAD), :] = jnp.zeros((PAD, CH), F32)
        dpad[r, pl.ds(PAD + W, PAD), :] = jnp.zeros((PAD, CH), F32)
    for r in range(R):
        mp[REACH + r, pl.ds(PAD, W), :] = maps_ref[r].astype(F32)

    HT = 256 if H % 256 == 0 else LANE
    cp_wp.wait()

    @pl.loop(0, H // HT)
    def _(j):
        o = pl.multiple_of(j * HT, HT)
        dact[:, pl.ds(o, HT)] = lax.dot_general(
            cot_ref[...], wp[pl.ds(o, HT), :], CONTRACT_LAST, preferred_element_type=F32
        )

    def fill(cond, copy, buf, target, base, width):
        @pl.when(cond)
        def _():
            copy.wait_recv()
            for r in range(REACH):
                if len(buf.shape) == 3:
                    target[base + r, pl.ds(PAD, W), :] = buf[r].astype(F32)
                else:
                    target[base + r, pl.ds(PAD, W), :] = buf[pl.ds(r * W, W), :].astype(F32)

        @pl.when(jnp.logical_not(cond))
        def _():
            for r in range(REACH):
                target[base + r, pl.ds(PAD, W), :] = jnp.zeros((W, width), F32)

    fill(has_lo, to_hi, halo_lo, mp, 0, C)
    fill(has_hi, to_lo, halo_hi, mp, REACH + R, C)

    @pl.loop(0, C // LANE)
    def _(t):
        o = pl.ds(pl.multiple_of(t * LANE, LANE), LANE)
        accs = [jnp.zeros((W, LANE), F32) for _ in range(R)]
        for b in range(KS):
            taps = [fil[pl.ds(a * KS + b, 1), o] for a in range(KS)]
            for rin in range(R + 2 * REACH):
                v = mp[rin, pl.ds(PAD - REACH + b, W), o]
                for r in range(R):
                    if 0 <= rin - r < KS:
                        accs[r] = accs[r] + v * taps[rin - r]
        for r in range(R):
            conv[pl.ds(r * W, W), o] = accs[r]

    @pl.loop(0, N // 16)
    def _(t):
        o = pl.ds(pl.multiple_of(t * 16, 16), 16)
        sc, inv = norm_stats(conv[o, :])
        scaled[o, :] = sc
        invs[o, :] = jnp.broadcast_to(inv, (16, LANE))
        nrm[0, o, :] = sc.astype(BF16)

    c_nrm = remote(nrm.at[0], nrm.at[1], s, pair_chip)
    c_nrm.start()

    cp_we.wait()

    @pl.loop(0, H // HT)
    def _(j):
        o = pl.ds(pl.multiple_of(j * HT, HT), HT)
        hid = jnp.dot(nrm[0], we[:, o], preferred_element_type=F32)
        a, slope = gelu_parts(hid)
        act[0, :, o] = a.astype(BF16)
        dh[0, :, o] = (dact[:, o] * slope).astype(BF16)

    c_pn = []
    for k in list(range(1, S)) + [0]:
        t = peers[k]
        pn[k] = lax.dot_general(
            dh[0], we[chan(t), :], CONTRACT_LAST, preferred_element_type=F32
        ).astype(BF16)
        if k:
            c = remote(pn.at[k], rn.at[k], t, d)
            c.start()
            c_pn.append(c)
    c_po = []
    for k in list(range(1, S)) + [0]:
        t = peers[k]
        po[k] = jnp.dot(act[0], wp[:, chan(t)], preferred_element_type=F32).astype(BF16)
        if k:
            c = remote(po.at[k], ro.at[k], t, d)
            c.start()
            c_po.append(c)

    c_cot.wait_recv()
    c_nrm.wait_recv()

    @pl.loop(0, H // HT)
    def _(j):
        o = pl.ds(pl.multiple_of(j * HT, HT), HT)
        hid = jnp.dot(nrm[1], we[:, o], preferred_element_type=F32)
        da = lax.dot_general(
            cots[...], wp[o, :], CONTRACT_LAST, preferred_element_type=F32
        )
        a, slope = gelu_parts(hid)
        act[1, :, o] = a.astype(BF16)
        dh[1, :, o] = (da * slope).astype(BF16)

    pc = dpcols(pair_core)
    mine = dpcols(d)
    c_core = [
        remote(act.at[pl.ds(0, 2)], act.at[pl.ds(2, 2)], s, pair_core),
        remote(dh.at[pl.ds(0, 2)], dh.at[pl.ds(2, 2)], s, pair_core),
        remote(nrm.at[pl.ds(0, 2), :, pc], ns.at[pl.ds(2, 2)], s, pair_core),
        remote(cot_ref.at[:, pc], cs.at[2], s, pair_core),
        remote(cots.at[:, pc], cs.at[3], s, pair_core),
    ]
    for c in c_core:
        c.start()
    ns[0] = nrm[0, :, mine]
    ns[1] = nrm[1, :, mine]
    cs[0] = cot_ref[:, mine]
    cs[1] = cots[:, mine]

    own = chan(s)
    for c in c_pn:
        c.wait_recv()
    dn = pn[0].astype(F32)
    for k in range(1, S):
        dn = dn + rn[k].astype(F32)
    sc = scaled[:, own]
    first = jnp.sum(dn, axis=-1, keepdims=True)
    second = jnp.sum(dn * sc, axis=-1, keepdims=True)
    lane = lax.broadcasted_iota(jnp.int32, (N, LANE), 1)
    st[...] = jnp.where(lane == 0, first, jnp.where(lane == 1, second, 0.0)).T[:8]
    c_st = []
    for k in range(1, S):
        c = remote(st, rst.at[k], peers[k], d)
        c.start()
        c_st.append(c)
    conv[:, pl.ds(0, CH)] = dn

    for c in c_po:
        c.wait_recv()
    for r in range(R):
        rows = pl.ds(r * W, W)
        total = po[0, rows, :].astype(F32)
        for k in range(1, S):
            total = total + ro[k, rows, :].astype(F32)
        bo[rows, :] = (mp[REACH + r, pl.ds(PAD, W), own] + total).astype(BF16)
    c_bo = []
    for k in range(1, S):
        c = remote(bo, out_hbm.at[:, own], peers[k], d)
        c.start()
        c_bo.append(c)
    l_bo = move(bo, out_hbm.at[:, own], 2)
    l_bo.start()

    for c in c_st:
        c.wait_recv()
    tot = st[...]
    for k in range(1, S):
        tot = tot + rst[k]
    tot = jnp.concatenate([tot, jnp.zeros((LANE - 8, N), F32)], axis=0).T * (1.0 / C)
    dcv[...] = (
        invs[:, pl.ds(0, 1)]
        * (conv[:, pl.ds(0, CH)] - tot[:, 0:1] - scaled[:, own] * tot[:, 1:2])
    ).astype(BF16)
    gto_hi = remote(dcv.at[pl.ds((R - REACH) * W, REACH * W)], dlo, s, hi_dp)
    gto_lo = remote(dcv.at[pl.ds(0, REACH * W)], dhi, s, lo_dp)

    @pl.when(has_hi)
    def _():
        gto_hi.start()

    @pl.when(has_lo)
    def _():
        gto_lo.start()

    for r in range(R):
        dpad[REACH + r, pl.ds(PAD, W), :] = dcv[pl.ds(r * W, W), :].astype(F32)

    fpart[...] = jnp.zeros_like(fpart)

    @pl.loop(0, CH // LANE)
    def _(t):
        o = pl.ds(pl.multiple_of(t * LANE, LANE), LANE)
        so = pl.ds(pl.multiple_of(s * CH + t * LANE, LANE), LANE)
        grads = [dpad[REACH + r, pl.ds(PAD, W), o] for r in range(R)]
        for b in range(KS):
            sums = [jnp.zeros((W, LANE), F32) for _ in range(KS)]
            for rin in range(R + 2 * REACH):
                v = mp[rin, pl.ds(PAD - REACH + b, W), so]
                for r in range(R):
                    if 0 <= rin - r < KS:
                        sums[rin - r] = sums[rin - r] + v * grads[r]
            for a in range(KS):
                fpart[pl.ds(a * KS + b, 1), o] = jnp.sum(sums[a], axis=0, keepdims=True)

    fsum[d] = fpart[...].astype(BF16)
    c_f = []
    for k in range(1, 4):
        c = remote(fsum.at[d], fsum.at[d], s, lax.rem(d + k, 4))
        c.start()
        c_f.append(c)

    fill(has_lo, gto_hi, dlo, dpad, 0, CH)
    fill(has_hi, gto_lo, dhi, dpad, REACH + R, CH)

    @pl.loop(0, CH // LANE)
    def _(t):
        o = pl.ds(pl.multiple_of(t * LANE, LANE), LANE)
        so = pl.ds(pl.multiple_of(s * CH + t * LANE, LANE), LANE)
        accs = [cot_ref[pl.ds(r * W, W), so].astype(F32) for r in range(R)]
        for b in range(KS):
            taps = [fil[pl.ds(a * KS + b, 1), so] for a in range(KS)]
            for rin in range(R + 2 * REACH):
                v = dpad[rin, pl.ds(PAD + REACH - b, W), o]
                for r in range(R):
                    a = r + 2 * REACH - rin
                    if 0 <= a < KS:
                        accs[r] = accs[r] + v * taps[a]
        for r in range(R):
            gi[pl.ds(r * W, W), o] = accs[r].astype(BF16)

    c_gi = []
    for k in range(1, S):
        c = remote(gi, gin_hbm.at[:, own], peers[k], d)
        c.start()
        c_gi.append(c)
    l_gi = move(gi, gin_hbm.at[:, own], 3)
    l_gi.start()

    for c in c_f:
        c.wait_recv()
    fa = (fsum[0].astype(F32) + fsum[1].astype(F32)) + (
        fsum[2].astype(F32) + fsum[3].astype(F32)
    )
    fall[s] = fa.astype(BF16)
    c_fa = []
    for k in range(1, S):
        c = remote(fall.at[s], fall.at[s], peers[k], d)
        c.start()
        c_fa.append(c)

    for c in c_core:
        c.wait_recv()

    @pl.loop(0, H // HT)
    def _(j):
        o = pl.ds(pl.multiple_of(j * HT, HT), HT)
        ge[:, o] = lax.dot_general(
            ns[...].reshape(4 * N, DC), dh[:, :, o].reshape(4 * N, HT),
            CONTRACT_FIRST, preferred_element_type=F32,
        )

    l_ge = move(ge, ge_hbm, 4)
    l_ge.start()

    @pl.loop(0, H // HT)
    def _(j):
        o = pl.ds(pl.multiple_of(j * HT, HT), HT)
        gp[o, :] = lax.dot_general(
            act[:, :, o].reshape(4 * N, HT), cs[...].reshape(4 * N, DC),
            CONTRACT_FIRST, preferred_element_type=F32,
        )

    l_gp = move(gp, gp_hbm, 5)
    l_gp.start()

    for c in c_fa:
        c.wait_recv()
    for t in range(S):
        gf_ref[:, pl.ds(t * CH, CH)] = fall[t, pl.ds(0, KS * KS), :].astype(F32)
    for c in c_bo + c_gi:
        c.wait_recv()
    for c in [c_cot, c_nrm] + c_pn + c_po + c_core + c_st + c_bo + c_f + c_gi + c_fa:
        c.wait_send()
    for c in (to_hi, gto_hi):
        @pl.when(has_hi)
        def _():
            c.wait_send()
    for c in (to_lo, gto_lo):
        @pl.when(has_lo)
        def _():
            c.wait_send()
    for c in (l_bo, l_gi, l_ge, l_gp):
        c.wait()


def kernel_body(maps_in, filters, w_expand, w_project, cotangent):
    R, W, C = maps_in.shape
    H = w_expand.shape[1]
    S = lax.axis_size("shard")
    N, CH, DC, RE = R * W, C // S, C // 4, R + 2 * REACH
    VM = pltpu.VMEM
    scratch = [
        VM((C, H), BF16), VM((H, C), BF16), VM((56, C), F32),
        VM((RE, W + 2 * PAD, C), F32),
        VM((REACH, W, C), BF16), VM((REACH, W, C), BF16),
        VM((N, C), F32), VM((N, C), F32), VM((N, LANE), F32), VM((N, H), F32),
        VM((2, N, C), BF16), VM((N, C), BF16),
        VM((4, N, H), BF16), VM((4, N, H), BF16),
        VM((4, N, DC), BF16), VM((4, N, DC), BF16),
        VM((S, N, CH), BF16), VM((S, N, CH), BF16),
        VM((S, N, CH), BF16), VM((S, N, CH), BF16),
        VM((N, CH), BF16), VM((8, N), F32), VM((S, 8, N), F32),
        VM((N, CH), BF16), VM((REACH * W, CH), BF16), VM((REACH * W, CH), BF16),
        VM((RE, W + 2 * PAD, CH), F32),
        VM((64, CH), F32), VM((4, 64, CH), BF16), VM((S, 64, CH), BF16),
        VM((N, CH), BF16), VM((DC, H), F32), VM((H, DC), F32),
        pltpu.SemaphoreType.DMA((48,)), pltpu.SemaphoreType.DMA((48,)),
        pltpu.SemaphoreType.DMA((8,)),
    ]
    vmem = pl.BlockSpec(memory_space=pltpu.VMEM)
    anys = pl.BlockSpec(memory_space=pl.ANY)
    out, gin, ge, gp, gf = pl.pallas_call(
        functools.partial(kernel, S, R, W, C, H),
        out_shape=(
            jax.ShapeDtypeStruct((N, C), BF16),
            jax.ShapeDtypeStruct((N, C), BF16),
            jax.ShapeDtypeStruct((DC, H), F32),
            jax.ShapeDtypeStruct((H, DC), F32),
            jax.ShapeDtypeStruct((KS * KS, C), F32),
        ),
        in_specs=[vmem, vmem, vmem, anys, anys],
        out_specs=(anys, anys, anys, anys, vmem),
        scratch_shapes=scratch,
        compiler_params=pltpu.CompilerParams(
            collective_id=0, has_side_effects=True, vmem_limit_bytes=52 * 1024 * 1024
        ),
    )(maps_in, filters, cotangent.reshape(N, C), w_expand, w_project)
    return (out.reshape(R, W, C), gin.reshape(R, W, C), ge, gp, gf)


def body(maps_in, filters, w_expand, w_project, cotangent):
    rows, cols, width = maps_in.shape
    hid = w_expand.shape[1]
    shards = lax.axis_size("shard")
    fits = (
        lax.axis_size("dp") == 4
        and width % (shards * LANE) == 0
        and width % (4 * LANE) == 0
        and hid % LANE == 0
        and shards > 1
        and rows >= REACH
        and rows * cols == LANE
        and cols % 16 == 0
    )
    run = kernel_body if fits else plain_body
    return run(maps_in, filters, w_expand, w_project, cotangent)


def solution(mesh):
    placed = (
        P(("groups", "dp"), None, None),
        P(),
        P(None, "shard"),
        P("shard", None),
        P(("groups", "dp"), None, None),
    )
    return jax.shard_map(
        body,
        mesh=mesh,
        in_specs=placed,
        out_specs=(
            P(("groups", "dp"), None, None),
            P(("groups", "dp"), None, None),
            P(("groups", "dp"), "shard"),
            P(("groups", "shard"), "dp"),
            P("groups", None),
        ),
        check_vma=False,
    )
```

```python
import functools

import jax
import jax.numpy as jnp
from jax import lax
from jax.experimental import pallas as pl
from jax.experimental.pallas import tpu as pltpu
from jax.sharding import PartitionSpec as P

KS = 7
REACH = KS // 2
LANE = 128
PAD = 8
F32 = jnp.float32
BF16 = jnp.bfloat16
MESH = pl.DeviceIdType.MESH


def extended(block, sides, width):
    for axis, dim in sides:
        count = lax.axis_size(axis)
        forward = [(i, i + 1) for i in range(count - 1)]
        backward = [(target, source) for source, target in forward]
        low = lax.ppermute(
            lax.slice_in_dim(block, block.shape[dim] - width, None, axis=dim), axis, forward
        )
        high = lax.ppermute(lax.slice_in_dim(block, 0, width, axis=dim), axis, backward)
        block = jnp.concatenate([low, block, high], axis=dim)
    return block


def gelu_parts(hidden):
    cdf = 0.5 * (1.0 + lax.erf(hidden * 0.7071067811865476))
    density = jnp.exp(-0.5 * hidden * hidden) * 0.3989422804014327
    return (hidden * cdf, cdf + hidden * density)


def norm_stats(conv_rows):
    centered = conv_rows - jnp.mean(conv_rows, axis=-1, keepdims=True)
    variance = jnp.mean(centered * centered, axis=-1, keepdims=True)
    inv_scale = lax.rsqrt(variance + 1e-06)
    return (centered * inv_scale, inv_scale)


def norm_back(d_normed, scaled, inv_scale):
    first = jnp.mean(d_normed, axis=-1, keepdims=True)
    second = jnp.mean(d_normed * scaled, axis=-1, keepdims=True)
    return inv_scale * (d_normed - first - scaled * second)


def plain_body(maps_in, filters, w_expand, w_project, cotangent):
    reach = KS // 2
    rows, cols, width = maps_in.shape
    count = rows * cols
    taps_f32 = filters.astype(jnp.float32)
    halo_in = extended(maps_in, (("dp", 0),), reach)
    padded_in = jnp.pad(halo_in, ((0, 0), (reach, reach), (0, 0)))
    conv_out = jnp.zeros((rows, cols, width), jnp.float32)
    for tap in range(KS * KS):
        tap_row, tap_col = divmod(tap, KS)
        conv_out = (
            conv_out
            + padded_in[tap_row : tap_row + rows, tap_col : tap_col + cols].astype(jnp.float32)
            * taps_f32[tap]
        )
    scaled, inv_scale = norm_stats(conv_out.reshape(count, width))
    normed = scaled.astype(jnp.bfloat16)
    hidden = jnp.dot(normed, w_expand, preferred_element_type=jnp.float32)
    activ, slope = gelu_parts(hidden)
    act = activ.astype(jnp.bfloat16)
    partial_out = jnp.dot(act, w_project, preferred_element_type=jnp.float32)
    cot_rows = cotangent.reshape(count, width)
    summed_out = lax.psum(partial_out.astype(jnp.bfloat16), "shard").astype(jnp.float32)
    d_act = lax.dot_general(
        cot_rows, w_project, (((1,), (1,)), ((), ())), preferred_element_type=jnp.float32
    )
    d_hidden = (d_act * slope).astype(jnp.bfloat16)
    grad_proj_local = lax.dot_general(
        act, cot_rows, (((0,), (0,)), ((), ())), preferred_element_type=jnp.float32
    )
    grad_exp_local = lax.dot_general(
        normed, d_hidden, (((0,), (0,)), ((), ())), preferred_element_type=jnp.float32
    )
    partial_norm = lax.dot_general(
        d_hidden, w_expand, (((1,), (1,)), ((), ())), preferred_element_type=jnp.float32
    )
    d_normed = lax.psum(partial_norm.astype(jnp.bfloat16), "shard").astype(jnp.float32)
    d_conv = norm_back(d_normed, scaled, inv_scale).astype(jnp.bfloat16)
    block_out = (
        (maps_in.reshape(count, width).astype(jnp.float32) + summed_out)
        .astype(jnp.bfloat16)
        .reshape(rows, cols, width)
    )
    grad_expand, grad_project = (
        lax.psum_scatter(
            grad_exp_local.astype(jnp.bfloat16), "dp", scatter_dimension=0, tiled=True
        ).astype(jnp.float32),
        lax.psum_scatter(
            grad_proj_local.astype(jnp.bfloat16), "dp", scatter_dimension=1, tiled=True
        ).astype(jnp.float32),
    )
    d_conv = d_conv.reshape(rows, cols, width)
    halo_grad = extended(d_conv, (("dp", 0),), reach)
    padded_grad = jnp.pad(halo_grad, ((0, 0), (reach, reach), (0, 0)))
    conv_grad = d_conv.astype(jnp.float32)
    back_sum = cotangent.astype(jnp.float32)
    filter_rows = []
    for tap in range(KS * KS):
        tap_row, tap_col = divmod(tap, KS)
        back_sum = (
            back_sum
            + padded_grad[
                2 * reach - tap_row : 2 * reach - tap_row + rows,
                2 * reach - tap_col : 2 * reach - tap_col + cols,
            ].astype(jnp.float32)
            * taps_f32[tap]
        )
        filter_rows.append(
            jnp.sum(
                conv_grad
                * padded_in[tap_row : tap_row + rows, tap_col : tap_col + cols].astype(jnp.float32),
                axis=(0, 1),
            )
        )
    grad_input = back_sum.astype(jnp.bfloat16)
    grad_filters = lax.psum(jnp.stack(filter_rows, axis=0).astype(jnp.bfloat16), "dp").astype(
        jnp.float32
    )
    return (block_out, grad_input, grad_expand, grad_project, grad_filters)


CONTRACT_LAST = (((1,), (1,)), ((), ()))
CONTRACT_FIRST = (((0,), (0,)), ((), ()))


def kernel(
    S, R, W, C, H,
    maps_hbm, fil_hbm, cot_hbm, we_hbm, wp_hbm,
    out_ref, gin_ref, ge, gp, gf_ref,
    maps_ref, fil_ref, cot_ref, we, wp, fil, mp, halo_lo, halo_hi, conv, scaled, invs, dact,
    nrm, cots, act, dh, ns, cs, pn, rn, po, ro, st, rst,
    dcv, dlo, dhi, dpad, fpart, fsum, fall,
    send, recv, loc,
):
    N = R * W
    CH = C // S
    DC = C // 4
    g = lax.axis_index("groups")
    s = lax.axis_index("shard")
    d = lax.axis_index("dp")
    pair_core = d + 1 - 2 * lax.rem(d, 2)
    pair_chip = lax.rem(d + 2, 4)
    peers = [lax.rem(s + k, S) for k in range(S)]
    has_lo = d > 0
    has_hi = d < 3

    def chan(i):
        return pl.ds(pl.multiple_of(i * CH, LANE), CH)

    def dpcols(i):
        return pl.ds(pl.multiple_of(i * DC, LANE), DC)

    counter = [0]

    def remote(src, dst, shard, dp):
        i = counter[0]
        counter[0] += 1
        return pltpu.make_async_remote_copy(
            src_ref=src, dst_ref=dst, send_sem=send.at[i], recv_sem=recv.at[i],
            device_id=(g, shard, dp), device_id_type=MESH,
        )

    def move(src, dst, i):
        return pltpu.make_async_copy(src, dst, loc.at[i])

    cp_wp = move(wp_hbm, wp, 0)
    cp_we = move(we_hbm, we, 1)
    cp_maps = move(maps_hbm, maps_ref, 2)
    cp_fil = move(fil_hbm, fil_ref, 3)
    cp_cot = move(cot_hbm, cot_ref, 4)
    cp_maps.start()
    cp_cot.start()
    cp_fil.start()
    cp_wp.start()
    cp_we.start()

    barrier = pltpu.get_barrier_semaphore()
    for k in range(1, S):
        pl.semaphore_signal(barrier, inc=1, device_id=(g, peers[k], d), device_id_type=MESH)
    for k in range(1, 4):
        pl.semaphore_signal(
            barrier, inc=1, device_id=(g, s, lax.rem(d + k, 4)), device_id_type=MESH
        )
    pl.semaphore_wait(barrier, S - 1 + 3)

    lo_dp = jnp.maximum(d - 1, 0)
    hi_dp = jnp.minimum(d + 1, 3)
    to_hi = remote(maps_hbm.at[pl.ds(R - REACH, REACH)], halo_lo, s, hi_dp)
    to_lo = remote(maps_hbm.at[pl.ds(0, REACH)], halo_hi, s, lo_dp)

    @pl.when(has_hi)
    def _():
        to_hi.start()

    @pl.when(has_lo)
    def _():
        to_lo.start()

    cp_maps.wait()
    cp_fil.wait()
    fil[pl.ds(0, KS * KS), :] = fil_ref[...].astype(F32)
    for r in range(R + 2 * REACH):
        mp[r, pl.ds(0, PAD), :] = jnp.zeros((PAD, C), F32)
        mp[r, pl.ds(PAD + W, PAD), :] = jnp.zeros((PAD, C), F32)
        dpad[r, pl.ds(0, PAD), :] = jnp.zeros((PAD, CH), F32)
        dpad[r, pl.ds(PAD + W, PAD), :] = jnp.zeros((PAD, CH), F32)
    for r in range(R):
        mp[REACH + r, pl.ds(PAD, W), :] = maps_ref[r].astype(F32)

    HT = 256 if H % 256 == 0 else LANE
    cp_cot.wait()
    cp_wp.wait()

    @pl.loop(0, H // HT)
    def _(j):
        o = pl.multiple_of(j * HT, HT)
        dact[:, pl.ds(o, HT)] = lax.dot_general(
            cot_ref[...], wp[pl.ds(o, HT), :], CONTRACT_LAST, preferred_element_type=F32
        )

    def fill(cond, copy, buf, target, base, width):
        @pl.when(cond)
        def _():
            copy.wait_recv()
            for r in range(REACH):
                if len(buf.shape) == 3:
                    target[base + r, pl.ds(PAD, W), :] = buf[r].astype(F32)
                else:
                    target[base + r, pl.ds(PAD, W), :] = buf[pl.ds(r * W, W), :].astype(F32)

        @pl.when(jnp.logical_not(cond))
        def _():
            for r in range(REACH):
                target[base + r, pl.ds(PAD, W), :] = jnp.zeros((W, width), F32)

    fill(has_lo, to_hi, halo_lo, mp, 0, C)
    fill(has_hi, to_lo, halo_hi, mp, REACH + R, C)
    c_cot = remote(cot_hbm, cots, s, pair_chip)
    c_cot.start()

    @pl.loop(0, C // LANE)
    def _(t):
        o = pl.ds(pl.multiple_of(t * LANE, LANE), LANE)
        accs = [jnp.zeros((W, LANE), F32) for _ in range(R)]
        for b in range(KS):
            taps = [fil[pl.ds(a * KS + b, 1), o] for a in range(KS)]
            for rin in range(R + 2 * REACH):
                v = mp[rin, pl.ds(PAD - REACH + b, W), o]
                for r in range(R):
                    if 0 <= rin - r < KS:
                        accs[r] = accs[r] + v * taps[rin - r]
        for r in range(R):
            conv[pl.ds(r * W, W), o] = accs[r]

    @pl.loop(0, N // 16)
    def _(t):
        o = pl.ds(pl.multiple_of(t * 16, 16), 16)
        sc, inv = norm_stats(conv[o, :])
        scaled[o, :] = sc
        invs[o, :] = jnp.broadcast_to(inv, (16, LANE))
        nrm[0, o, :] = sc.astype(BF16)

    c_nrm = remote(nrm.at[0], nrm.at[1], s, pair_chip)
    c_nrm.start()

    cp_we.wait()

    @pl.loop(0, H // HT)
    def _(j):
        o = pl.ds(pl.multiple_of(j * HT, HT), HT)
        hid = jnp.dot(nrm[0], we[:, o], preferred_element_type=F32)
        a, slope = gelu_parts(hid)
        act[0, :, o] = a.astype(BF16)
        dh[0, :, o] = (dact[:, o] * slope).astype(BF16)

    c_pn = []
    for k in list(range(1, S)) + [0]:
        t = peers[k]
        pn[k] = lax.dot_general(
            dh[0], we[chan(t), :], CONTRACT_LAST, preferred_element_type=F32
        ).astype(BF16)
        if k:
            c = remote(pn.at[k], rn.at[k], t, d)
            c.start()
            c_pn.append(c)
    c_po = []
    for k in list(range(1, S)) + [0]:
        t = peers[k]
        po[k] = jnp.dot(act[0], wp[:, chan(t)], preferred_element_type=F32).astype(BF16)
        if k:
            c_po.append(remote(po.at[k], ro.at[k], t, d))

    c_cot.wait_recv()
    c_nrm.wait_recv()

    @pl.loop(0, H // HT)
    def _(j):
        o = pl.ds(pl.multiple_of(j * HT, HT), HT)
        hid = jnp.dot(nrm[1], we[:, o], preferred_element_type=F32)
        da = lax.dot_general(
            cots[...], wp[o, :], CONTRACT_LAST, preferred_element_type=F32
        )
        a, slope = gelu_parts(hid)
        act[1, :, o] = a.astype(BF16)
        dh[1, :, o] = (da * slope).astype(BF16)

    pc = dpcols(pair_core)
    mine = dpcols(d)
    c_core = [
        remote(act.at[pl.ds(0, 2)], act.at[pl.ds(2, 2)], s, pair_core),
        remote(dh.at[pl.ds(0, 2)], dh.at[pl.ds(2, 2)], s, pair_core),
        remote(nrm.at[pl.ds(0, 2), :, pc], ns.at[pl.ds(2, 2)], s, pair_core),
        remote(cot_ref.at[:, pc], cs.at[2], s, pair_core),
        remote(cots.at[:, pc], cs.at[3], s, pair_core),
    ]
    for c in c_core:
        c.start()
    ns[0] = nrm[0, :, mine]
    ns[1] = nrm[1, :, mine]
    cs[0] = cot_ref[:, mine]
    cs[1] = cots[:, mine]

    own = chan(s)
    for c in c_pn:
        c.wait_recv()
    dn = pn[0].astype(F32)
    for k in range(1, S):
        dn = dn + rn[k].astype(F32)
    sc = scaled[:, own]
    first = jnp.sum(dn, axis=-1, keepdims=True)
    second = jnp.sum(dn * sc, axis=-1, keepdims=True)
    lane = lax.broadcasted_iota(jnp.int32, (N, LANE), 1)
    st[...] = jnp.where(lane == 0, first, jnp.where(lane == 1, second, 0.0)).T[:8]
    c_st = []
    for k in range(1, S):
        c = remote(st, rst.at[k], peers[k], d)
        c.start()
        c_st.append(c)
    conv[:, pl.ds(0, CH)] = dn

    for c in c_po:
        c.start()

    for c in c_st:
        c.wait_recv()
    tot = st[...]
    for k in range(1, S):
        tot = tot + rst[k]
    tot = jnp.concatenate([tot, jnp.zeros((LANE - 8, N), F32)], axis=0).T * (1.0 / C)
    dcv[...] = (
        invs[:, pl.ds(0, 1)]
        * (conv[:, pl.ds(0, CH)] - tot[:, 0:1] - scaled[:, own] * tot[:, 1:2])
    ).astype(BF16)
    gto_hi = remote(dcv.at[pl.ds((R - REACH) * W, REACH * W)], dlo, s, hi_dp)
    gto_lo = remote(dcv.at[pl.ds(0, REACH * W)], dhi, s, lo_dp)

    @pl.when(has_hi)
    def _():
        gto_hi.start()

    @pl.when(has_lo)
    def _():
        gto_lo.start()

    for r in range(R):
        dpad[REACH + r, pl.ds(PAD, W), :] = dcv[pl.ds(r * W, W), :].astype(F32)

    fpart[...] = jnp.zeros_like(fpart)

    @pl.loop(0, CH // LANE)
    def _(t):
        o = pl.ds(pl.multiple_of(t * LANE, LANE), LANE)
        so = pl.ds(pl.multiple_of(s * CH + t * LANE, LANE), LANE)
        grads = [dpad[REACH + r, pl.ds(PAD, W), o] for r in range(R)]
        for b in range(KS):
            sums = [jnp.zeros((W, LANE), F32) for _ in range(KS)]
            for rin in range(R + 2 * REACH):
                v = mp[rin, pl.ds(PAD - REACH + b, W), so]
                for r in range(R):
                    if 0 <= rin - r < KS:
                        sums[rin - r] = sums[rin - r] + v * grads[r]
            for a in range(KS):
                fpart[pl.ds(a * KS + b, 1), o] = jnp.sum(sums[a], axis=0, keepdims=True)

    fsum[d] = fpart[...].astype(BF16)
    c_f = []
    for k in range(1, 4):
        c = remote(fsum.at[d], fsum.at[d], s, lax.rem(d + k, 4))
        c.start()
        c_f.append(c)

    fill(has_lo, gto_hi, dlo, dpad, 0, CH)
    fill(has_hi, gto_lo, dhi, dpad, REACH + R, CH)

    @pl.loop(0, CH // LANE)
    def _(t):
        o = pl.ds(pl.multiple_of(t * LANE, LANE), LANE)
        so = pl.ds(pl.multiple_of(s * CH + t * LANE, LANE), LANE)
        accs = [cot_ref[pl.ds(r * W, W), so].astype(F32) for r in range(R)]
        for b in range(KS):
            taps = [fil[pl.ds(a * KS + b, 1), so] for a in range(KS)]
            for rin in range(R + 2 * REACH):
                v = dpad[rin, pl.ds(PAD + REACH - b, W), o]
                for r in range(R):
                    a = r + 2 * REACH - rin
                    if 0 <= a < KS:
                        accs[r] = accs[r] + v * taps[a]
        for r in range(R):
            gin_ref[pl.ds(r * W, W), so] = accs[r].astype(BF16)

    c_gi = []
    for k in range(1, S):
        c = remote(gin_ref.at[:, own], gin_ref.at[:, own], peers[k], d)
        c.start()
        c_gi.append(c)

    for c in c_po:
        c.wait_recv()
    for r in range(R):
        rows = pl.ds(r * W, W)
        total = po[0, rows, :].astype(F32)
        for k in range(1, S):
            total = total + ro[k, rows, :].astype(F32)
        out_ref[rows, own] = (mp[REACH + r, pl.ds(PAD, W), own] + total).astype(BF16)
    c_bo = []
    for k in range(1, S):
        c = remote(out_ref.at[:, own], out_ref.at[:, own], peers[k], d)
        c.start()
        c_bo.append(c)

    for c in c_f:
        c.wait_recv()
    fa = (fsum[0].astype(F32) + fsum[1].astype(F32)) + (
        fsum[2].astype(F32) + fsum[3].astype(F32)
    )
    fall[s] = fa.astype(BF16)
    c_fa = []
    for k in range(1, S):
        c = remote(fall.at[s], fall.at[s], peers[k], d)
        c.start()
        c_fa.append(c)

    for c in c_core:
        c.wait_recv()

    @pl.loop(0, H // HT)
    def _(j):
        o = pl.ds(pl.multiple_of(j * HT, HT), HT)
        ge[:, o] = lax.dot_general(
            ns[...].reshape(4 * N, DC), dh[:, :, o].reshape(4 * N, HT),
            CONTRACT_FIRST, preferred_element_type=F32,
        )


    @pl.loop(0, H // HT)
    def _(j):
        o = pl.ds(pl.multiple_of(j * HT, HT), HT)
        gp[o, :] = lax.dot_general(
            act[:, :, o].reshape(4 * N, HT), cs[...].reshape(4 * N, DC),
            CONTRACT_FIRST, preferred_element_type=F32,
        )


    for c in c_fa:
        c.wait_recv()
    for t in range(S):
        gf_ref[:, pl.ds(t * CH, CH)] = fall[t, pl.ds(0, KS * KS), :].astype(F32)
    for c in c_bo + c_gi:
        c.wait_recv()
    for c in [c_cot, c_nrm] + c_pn + c_po + c_core + c_st + c_bo + c_f + c_gi + c_fa:
        c.wait_send()
    for c in (to_hi, gto_hi):
        @pl.when(has_hi)
        def _():
            c.wait_send()
    for c in (to_lo, gto_lo):
        @pl.when(has_lo)
        def _():
            c.wait_send()


def store_kernel(*refs):
    sems = refs[-1]
    half = (len(refs) - 1) // 2
    copies = [
        pltpu.make_async_copy(refs[i], refs[half + i], sems.at[i]) for i in range(half)
    ]
    for c in copies:
        c.start()
    for c in copies:
        c.wait()


def kernel_body(maps_in, filters, w_expand, w_project, cotangent):
    R, W, C = maps_in.shape
    H = w_expand.shape[1]
    S = lax.axis_size("shard")
    N, CH, DC, RE = R * W, C // S, C // 4, R + 2 * REACH
    VM = pltpu.VMEM
    scratch = [
        VM((R, W, C), BF16), VM((KS * KS, C), BF16), VM((N, C), BF16),
        VM((C, H), BF16), VM((H, C), BF16), VM((56, C), F32),
        VM((RE, W + 2 * PAD, C), F32),
        VM((REACH, W, C), BF16), VM((REACH, W, C), BF16),
        VM((N, C), F32), VM((N, C), F32), VM((N, LANE), F32), VM((N, H), F32),
        VM((2, N, C), BF16), VM((N, C), BF16),
        VM((4, N, H), BF16), VM((4, N, H), BF16),
        VM((4, N, DC), BF16), VM((4, N, DC), BF16),
        VM((S, N, CH), BF16), VM((S, N, CH), BF16),
        VM((S, N, CH), BF16), VM((S, N, CH), BF16),
        VM((8, N), F32), VM((S, 8, N), F32),
        VM((N, CH), BF16), VM((REACH * W, CH), BF16), VM((REACH * W, CH), BF16),
        VM((RE, W + 2 * PAD, CH), F32),
        VM((64, CH), F32), VM((4, 64, CH), BF16), VM((S, 64, CH), BF16),
        pltpu.SemaphoreType.DMA((48,)), pltpu.SemaphoreType.DMA((48,)),
        pltpu.SemaphoreType.DMA((8,)),
    ]
    vmem = pl.BlockSpec(memory_space=pltpu.VMEM)
    anys = pl.BlockSpec(memory_space=pl.ANY)
    shapes = (
        jax.ShapeDtypeStruct((N, C), BF16),
        jax.ShapeDtypeStruct((N, C), BF16),
        jax.ShapeDtypeStruct((DC, H), F32),
        jax.ShapeDtypeStruct((H, DC), F32),
        jax.ShapeDtypeStruct((KS * KS, C), F32),
    )
    results = pl.pallas_call(
        functools.partial(kernel, S, R, W, C, H),
        out_shape=shapes,
        in_specs=[pl.BlockSpec(memory_space=pltpu.HBM)] * 5,
        out_specs=(vmem,) * 5,
        scratch_shapes=scratch,
        compiler_params=pltpu.CompilerParams(
            collective_id=0, has_side_effects=True, vmem_limit_bytes=44 * 1024 * 1024
        ),
    )(maps_in, filters, cotangent.reshape(N, C), w_expand, w_project)
    out, gin, ge, gp, gf = pl.pallas_call(
        store_kernel,
        out_shape=shapes,
        in_specs=[anys] * 5,
        out_specs=(anys,) * 5,
        scratch_shapes=[pltpu.SemaphoreType.DMA((5,))],
        compiler_params=pltpu.CompilerParams(vmem_limit_bytes=1024 * 1024),
    )(*results)
    return (out.reshape(R, W, C), gin.reshape(R, W, C), ge, gp, gf)


def body(maps_in, filters, w_expand, w_project, cotangent):
    rows, cols, width = maps_in.shape
    hid = w_expand.shape[1]
    shards = lax.axis_size("shard")
    fits = (
        lax.axis_size("dp") == 4
        and width % (shards * LANE) == 0
        and width % (4 * LANE) == 0
        and hid % LANE == 0
        and shards > 1
        and rows >= REACH
        and rows * cols == LANE
        and cols % 16 == 0
    )
    run = kernel_body if fits else plain_body
    return run(maps_in, filters, w_expand, w_project, cotangent)


def solution(mesh):
    placed = (
        P(("groups", "dp"), None, None),
        P(),
        P(None, "shard"),
        P("shard", None),
        P(("groups", "dp"), None, None),
    )
    return jax.shard_map(
        body,
        mesh=mesh,
        in_specs=placed,
        out_specs=(
            P(("groups", "dp"), None, None),
            P(("groups", "dp"), None, None),
            P(("groups", "dp"), "shard"),
            P(("groups", "shard"), "dp"),
            P("groups", None),
        ),
        check_vma=False,
    )
```

```python
import functools

import jax
import jax.numpy as jnp
from jax import lax
from jax.experimental import pallas as pl
from jax.experimental.pallas import tpu as pltpu
from jax.sharding import PartitionSpec as P

KS = 7
REACH = KS // 2
LANE = 128
PAD = 8
F32 = jnp.float32
BF16 = jnp.bfloat16
MESH = pl.DeviceIdType.MESH


def extended(block, sides, width):
    for axis, dim in sides:
        count = lax.axis_size(axis)
        forward = [(i, i + 1) for i in range(count - 1)]
        backward = [(target, source) for source, target in forward]
        low = lax.ppermute(
            lax.slice_in_dim(block, block.shape[dim] - width, None, axis=dim), axis, forward
        )
        high = lax.ppermute(lax.slice_in_dim(block, 0, width, axis=dim), axis, backward)
        block = jnp.concatenate([low, block, high], axis=dim)
    return block


def gelu_parts(hidden):
    cdf = 0.5 * (1.0 + lax.erf(hidden * 0.7071067811865476))
    density = jnp.exp(-0.5 * hidden * hidden) * 0.3989422804014327
    return (hidden * cdf, cdf + hidden * density)


def norm_stats(conv_rows):
    centered = conv_rows - jnp.mean(conv_rows, axis=-1, keepdims=True)
    variance = jnp.mean(centered * centered, axis=-1, keepdims=True)
    inv_scale = lax.rsqrt(variance + 1e-06)
    return (centered * inv_scale, inv_scale)


def norm_back(d_normed, scaled, inv_scale):
    first = jnp.mean(d_normed, axis=-1, keepdims=True)
    second = jnp.mean(d_normed * scaled, axis=-1, keepdims=True)
    return inv_scale * (d_normed - first - scaled * second)


def plain_body(maps_in, filters, w_expand, w_project, cotangent):
    reach = KS // 2
    rows, cols, width = maps_in.shape
    count = rows * cols
    taps_f32 = filters.astype(jnp.float32)
    halo_in = extended(maps_in, (("dp", 0),), reach)
    padded_in = jnp.pad(halo_in, ((0, 0), (reach, reach), (0, 0)))
    conv_out = jnp.zeros((rows, cols, width), jnp.float32)
    for tap in range(KS * KS):
        tap_row, tap_col = divmod(tap, KS)
        conv_out = (
            conv_out
            + padded_in[tap_row : tap_row + rows, tap_col : tap_col + cols].astype(jnp.float32)
            * taps_f32[tap]
        )
    scaled, inv_scale = norm_stats(conv_out.reshape(count, width))
    normed = scaled.astype(jnp.bfloat16)
    hidden = jnp.dot(normed, w_expand, preferred_element_type=jnp.float32)
    activ, slope = gelu_parts(hidden)
    act = activ.astype(jnp.bfloat16)
    partial_out = jnp.dot(act, w_project, preferred_element_type=jnp.float32)
    cot_rows = cotangent.reshape(count, width)
    summed_out = lax.psum(partial_out.astype(jnp.bfloat16), "shard").astype(jnp.float32)
    d_act = lax.dot_general(
        cot_rows, w_project, (((1,), (1,)), ((), ())), preferred_element_type=jnp.float32
    )
    d_hidden = (d_act * slope).astype(jnp.bfloat16)
    grad_proj_local = lax.dot_general(
        act, cot_rows, (((0,), (0,)), ((), ())), preferred_element_type=jnp.float32
    )
    grad_exp_local = lax.dot_general(
        normed, d_hidden, (((0,), (0,)), ((), ())), preferred_element_type=jnp.float32
    )
    partial_norm = lax.dot_general(
        d_hidden, w_expand, (((1,), (1,)), ((), ())), preferred_element_type=jnp.float32
    )
    d_normed = lax.psum(partial_norm.astype(jnp.bfloat16), "shard").astype(jnp.float32)
    d_conv = norm_back(d_normed, scaled, inv_scale).astype(jnp.bfloat16)
    block_out = (
        (maps_in.reshape(count, width).astype(jnp.float32) + summed_out)
        .astype(jnp.bfloat16)
        .reshape(rows, cols, width)
    )
    grad_expand, grad_project = (
        lax.psum_scatter(
            grad_exp_local.astype(jnp.bfloat16), "dp", scatter_dimension=0, tiled=True
        ).astype(jnp.float32),
        lax.psum_scatter(
            grad_proj_local.astype(jnp.bfloat16), "dp", scatter_dimension=1, tiled=True
        ).astype(jnp.float32),
    )
    d_conv = d_conv.reshape(rows, cols, width)
    halo_grad = extended(d_conv, (("dp", 0),), reach)
    padded_grad = jnp.pad(halo_grad, ((0, 0), (reach, reach), (0, 0)))
    conv_grad = d_conv.astype(jnp.float32)
    back_sum = cotangent.astype(jnp.float32)
    filter_rows = []
    for tap in range(KS * KS):
        tap_row, tap_col = divmod(tap, KS)
        back_sum = (
            back_sum
            + padded_grad[
                2 * reach - tap_row : 2 * reach - tap_row + rows,
                2 * reach - tap_col : 2 * reach - tap_col + cols,
            ].astype(jnp.float32)
            * taps_f32[tap]
        )
        filter_rows.append(
            jnp.sum(
                conv_grad
                * padded_in[tap_row : tap_row + rows, tap_col : tap_col + cols].astype(jnp.float32),
                axis=(0, 1),
            )
        )
    grad_input = back_sum.astype(jnp.bfloat16)
    grad_filters = lax.psum(jnp.stack(filter_rows, axis=0).astype(jnp.bfloat16), "dp").astype(
        jnp.float32
    )
    return (block_out, grad_input, grad_expand, grad_project, grad_filters)


CONTRACT_LAST = (((1,), (1,)), ((), ()))
CONTRACT_FIRST = (((0,), (0,)), ((), ()))


def kernel(
    S, R, W, C, H,
    maps_hbm, fil_hbm, cot_hbm, we_hbm, wp_hbm,
    out_ref, gin_ref, ge, gp, gf_ref,
    maps_ref, fil_ref, cot_ref, we, wp, fil, mp, halo_lo, halo_hi, conv, scaled, invs, dact,
    nrm, cots, act, dh, ns, cs, pn, rn, po, ro, st, rst,
    dcv, dlo, dhi, dpad, fpart, fsend, fsum, fall,
    send, recv, loc,
):
    N = R * W
    CH = C // S
    DC = C // 4
    g = lax.axis_index("groups")
    s = lax.axis_index("shard")
    d = lax.axis_index("dp")
    pair_core = d + 1 - 2 * lax.rem(d, 2)
    pair_chip = lax.rem(d + 2, 4)
    peers = [lax.rem(s + k, S) for k in range(S)]
    has_lo = d > 0
    has_hi = d < 3

    def chan(i):
        return pl.ds(pl.multiple_of(i * CH, LANE), CH)

    def dpcols(i):
        return pl.ds(pl.multiple_of(i * DC, LANE), DC)

    counter = [0]

    def remote(src, dst, shard, dp):
        i = counter[0]
        counter[0] += 1
        return pltpu.make_async_remote_copy(
            src_ref=src, dst_ref=dst, send_sem=send.at[i], recv_sem=recv.at[i],
            device_id=(g, shard, dp), device_id_type=MESH,
        )

    def move(src, dst, i):
        return pltpu.make_async_copy(src, dst, loc.at[i])

    cp_wp = move(wp_hbm, wp, 0)
    cp_we = move(we_hbm, we, 1)
    cp_maps = move(maps_hbm, maps_ref, 2)
    cp_fil = move(fil_hbm, fil_ref, 3)
    cp_cot = move(cot_hbm, cot_ref, 4)
    cp_maps.start()
    cp_cot.start()
    cp_fil.start()
    cp_wp.start()
    cp_we.start()

    barrier = pltpu.get_barrier_semaphore()
    for k in range(1, S):
        pl.semaphore_signal(barrier, inc=1, device_id=(g, peers[k], d), device_id_type=MESH)
    for k in range(1, 4):
        pl.semaphore_signal(
            barrier, inc=1, device_id=(g, s, lax.rem(d + k, 4)), device_id_type=MESH
        )
    pl.semaphore_wait(barrier, S - 1 + 3)

    lo_dp = jnp.maximum(d - 1, 0)
    hi_dp = jnp.minimum(d + 1, 3)
    to_hi = remote(maps_hbm.at[pl.ds(R - REACH, REACH)], halo_lo, s, hi_dp)
    to_lo = remote(maps_hbm.at[pl.ds(0, REACH)], halo_hi, s, lo_dp)

    @pl.when(has_hi)
    def _():
        to_hi.start()

    @pl.when(has_lo)
    def _():
        to_lo.start()

    cp_maps.wait()
    cp_fil.wait()
    fil[pl.ds(0, KS * KS), :] = fil_ref[...].astype(F32)
    for r in range(R + 2 * REACH):
        mp[r, pl.ds(0, PAD), :] = jnp.zeros((PAD, C), F32)
        mp[r, pl.ds(PAD + W, PAD), :] = jnp.zeros((PAD, C), F32)
        dpad[r, pl.ds(0, PAD), :] = jnp.zeros((PAD, CH), F32)
        dpad[r, pl.ds(PAD + W, PAD), :] = jnp.zeros((PAD, CH), F32)
    for r in range(R):
        mp[REACH + r, pl.ds(PAD, W), :] = maps_ref[r].astype(F32)

    HT = 256 if H % 256 == 0 else LANE
    cp_cot.wait()
    cp_wp.wait()

    @pl.loop(0, H // HT)
    def _(j):
        o = pl.multiple_of(j * HT, HT)
        dact[:, pl.ds(o, HT)] = lax.dot_general(
            cot_ref[...], wp[pl.ds(o, HT), :], CONTRACT_LAST, preferred_element_type=F32
        )

    def fill(cond, copy, buf, target, base, width):
        @pl.when(cond)
        def _():
            copy.wait_recv()
            for r in range(REACH):
                if len(buf.shape) == 3:
                    target[base + r, pl.ds(PAD, W), :] = buf[r].astype(F32)
                else:
                    target[base + r, pl.ds(PAD, W), :] = buf[pl.ds(r * W, W), :].astype(F32)

        @pl.when(jnp.logical_not(cond))
        def _():
            for r in range(REACH):
                target[base + r, pl.ds(PAD, W), :] = jnp.zeros((W, width), F32)

    fill(has_lo, to_hi, halo_lo, mp, 0, C)
    fill(has_hi, to_lo, halo_hi, mp, REACH + R, C)
    c_cot = remote(cot_hbm, cots, s, pair_chip)
    c_cot.start()

    @pl.loop(0, C // LANE)
    def _(t):
        o = pl.ds(pl.multiple_of(t * LANE, LANE), LANE)
        accs = [jnp.zeros((W, LANE), F32) for _ in range(R)]
        for b in range(KS):
            taps = [fil[pl.ds(a * KS + b, 1), o] for a in range(KS)]
            for rin in range(R + 2 * REACH):
                v = mp[rin, pl.ds(PAD - REACH + b, W), o]
                for r in range(R):
                    if 0 <= rin - r < KS:
                        accs[r] = accs[r] + v * taps[rin - r]
        for r in range(R):
            conv[pl.ds(r * W, W), o] = accs[r]

    @pl.loop(0, N // 16)
    def _(t):
        o = pl.ds(pl.multiple_of(t * 16, 16), 16)
        sc, inv = norm_stats(conv[o, :])
        scaled[o, :] = sc
        invs[o, :] = jnp.broadcast_to(inv, (16, LANE))
        nrm[0, o, :] = sc.astype(BF16)

    c_nrm = remote(nrm.at[0], nrm.at[1], s, pair_chip)
    c_nrm.start()

    cp_we.wait()

    @pl.loop(0, H // HT)
    def _(j):
        o = pl.ds(pl.multiple_of(j * HT, HT), HT)
        hid = jnp.dot(nrm[0], we[:, o], preferred_element_type=F32)
        a, slope = gelu_parts(hid)
        act[0, :, o] = a.astype(BF16)
        dh[0, :, o] = (dact[:, o] * slope).astype(BF16)

    c_pn = []
    for k in list(range(1, S)) + [0]:
        t = peers[k]
        pn[k] = lax.dot_general(
            dh[0], we[chan(t), :], CONTRACT_LAST, preferred_element_type=F32
        ).astype(BF16)
        if k:
            c = remote(pn.at[k], rn.at[k], t, d)
            c.start()
            c_pn.append(c)
    c_po = []
    for k in list(range(1, S)) + [0]:
        t = peers[k]
        po[k] = jnp.dot(act[0], wp[:, chan(t)], preferred_element_type=F32).astype(BF16)
        if k:
            c_po.append(remote(po.at[k], ro.at[k], t, d))

    c_cot.wait_recv()

    @pl.loop(0, H // HT)
    def _(j):
        o = pl.multiple_of(j * HT, HT)
        dact[:, pl.ds(o, HT)] = lax.dot_general(
            cots[...], wp[pl.ds(o, HT), :], CONTRACT_LAST, preferred_element_type=F32
        )

    own = chan(s)
    for c in c_pn:
        c.wait_recv()
    dn = pn[0].astype(F32)
    for k in range(1, S):
        dn = dn + rn[k].astype(F32)
    sc = scaled[:, own]
    first = jnp.sum(dn, axis=-1, keepdims=True)
    second = jnp.sum(dn * sc, axis=-1, keepdims=True)
    lane = lax.broadcasted_iota(jnp.int32, (N, LANE), 1)
    st[...] = jnp.where(lane == 0, first, jnp.where(lane == 1, second, 0.0)).T[:8]
    c_st = []
    for k in range(1, S):
        c = remote(st, rst.at[k], peers[k], d)
        c.start()
        c_st.append(c)
    conv[:, pl.ds(0, CH)] = dn

    for c in c_po:
        c.start()

    for c in c_st:
        c.wait_recv()
    tot = st[...]
    for k in range(1, S):
        tot = tot + rst[k]
    tot = jnp.concatenate([tot, jnp.zeros((LANE - 8, N), F32)], axis=0).T * (1.0 / C)
    dcv[...] = (
        invs[:, pl.ds(0, 1)]
        * (conv[:, pl.ds(0, CH)] - tot[:, 0:1] - scaled[:, own] * tot[:, 1:2])
    ).astype(BF16)
    gto_hi = remote(dcv.at[pl.ds((R - REACH) * W, REACH * W)], dlo, s, hi_dp)
    gto_lo = remote(dcv.at[pl.ds(0, REACH * W)], dhi, s, lo_dp)

    @pl.when(has_hi)
    def _():
        gto_hi.start()

    @pl.when(has_lo)
    def _():
        gto_lo.start()

    for r in range(R):
        dpad[REACH + r, pl.ds(PAD, W), :] = dcv[pl.ds(r * W, W), :].astype(F32)

    fpart[...] = jnp.zeros_like(fpart)

    @pl.loop(0, CH // LANE)
    def _(t):
        o = pl.ds(pl.multiple_of(t * LANE, LANE), LANE)
        so = pl.ds(pl.multiple_of(s * CH + t * LANE, LANE), LANE)
        grads = [dpad[REACH + r, pl.ds(PAD, W), o] for r in range(R)]
        for b in range(KS):
            sums = [jnp.zeros((W, LANE), F32) for _ in range(KS)]
            for rin in range(R + 2 * REACH):
                v = mp[rin, pl.ds(PAD - REACH + b, W), so]
                for r in range(R):
                    if 0 <= rin - r < KS:
                        sums[rin - r] = sums[rin - r] + v * grads[r]
            for a in range(KS):
                fpart[pl.ds(a * KS + b, 1), o] = jnp.sum(sums[a], axis=0, keepdims=True)

    fsend[...] = fpart[...].astype(BF16)
    fsum[d] = fsend[pl.ds(pl.multiple_of(d * 16, 16), 16), :]
    c_f = []
    for k in range(1, 4):
        t = lax.rem(d + k, 4)
        c = remote(
            fsend.at[pl.ds(pl.multiple_of(t * 16, 16), 16)], fsum.at[d], s, t
        )
        c.start()
        c_f.append(c)

    fill(has_lo, gto_hi, dlo, dpad, 0, CH)
    fill(has_hi, gto_lo, dhi, dpad, REACH + R, CH)

    @pl.loop(0, CH // LANE)
    def _(t):
        o = pl.ds(pl.multiple_of(t * LANE, LANE), LANE)
        so = pl.ds(pl.multiple_of(s * CH + t * LANE, LANE), LANE)
        accs = [cot_ref[pl.ds(r * W, W), so].astype(F32) for r in range(R)]
        for b in range(KS):
            taps = [fil[pl.ds(a * KS + b, 1), so] for a in range(KS)]
            for rin in range(R + 2 * REACH):
                v = dpad[rin, pl.ds(PAD + REACH - b, W), o]
                for r in range(R):
                    a = r + 2 * REACH - rin
                    if 0 <= a < KS:
                        accs[r] = accs[r] + v * taps[a]
        for r in range(R):
            gin_ref[pl.ds(r * W, W), so] = accs[r].astype(BF16)

    c_gi = []
    for k in range(1, S):
        c = remote(gin_ref.at[:, own], gin_ref.at[:, own], peers[k], d)
        c.start()
        c_gi.append(c)

    for c in c_f:
        c.wait_recv()
    fa = (fsum[0].astype(F32) + fsum[1].astype(F32)) + (
        fsum[2].astype(F32) + fsum[3].astype(F32)
    )
    fall[d, s] = fa.astype(BF16)
    c_fz = []
    for k in range(1, S):
        c = remote(fall.at[d, s], fall.at[d, s], peers[k], d)
        c.start()
        c_fz.append(c)

    for c in c_po:
        c.wait_recv()
    for r in range(R):
        rows = pl.ds(r * W, W)
        total = po[0, rows, :].astype(F32)
        for k in range(1, S):
            total = total + ro[k, rows, :].astype(F32)
        out_ref[rows, own] = (mp[REACH + r, pl.ds(PAD, W), own] + total).astype(BF16)
    c_bo = []
    for k in range(1, S):
        c = remote(out_ref.at[:, own], out_ref.at[:, own], peers[k], d)
        c.start()
        c_bo.append(c)

    c_nrm.wait_recv()

    @pl.loop(0, H // HT)
    def _(j):
        o = pl.ds(pl.multiple_of(j * HT, HT), HT)
        hid = jnp.dot(nrm[1], we[:, o], preferred_element_type=F32)
        a, slope = gelu_parts(hid)
        act[1, :, o] = a.astype(BF16)
        dh[1, :, o] = (dact[:, o] * slope).astype(BF16)

    pc = dpcols(pair_core)
    mine = dpcols(d)
    c_core = [
        remote(act.at[pl.ds(0, 2)], act.at[pl.ds(2, 2)], s, pair_core),
        remote(dh.at[pl.ds(0, 2)], dh.at[pl.ds(2, 2)], s, pair_core),
        remote(nrm.at[pl.ds(0, 2), :, pc], ns.at[pl.ds(2, 2)], s, pair_core),
        remote(cot_ref.at[:, pc], cs.at[2], s, pair_core),
        remote(cots.at[:, pc], cs.at[3], s, pair_core),
    ]
    for c in c_core:
        c.start()
    ns[0] = nrm[0, :, mine]
    ns[1] = nrm[1, :, mine]
    cs[0] = cot_ref[:, mine]
    cs[1] = cots[:, mine]

    for c in c_fz:
        c.wait_recv()
    c_fa = []
    for k in range(1, 4):
        c = remote(fall.at[d], fall.at[d], s, lax.rem(d + k, 4))
        c.start()
        c_fa.append(c)

    for c in c_core:
        c.wait_recv()

    @pl.loop(0, H // HT)
    def _(j):
        o = pl.ds(pl.multiple_of(j * HT, HT), HT)
        ge[:, o] = lax.dot_general(
            ns[...].reshape(4 * N, DC), dh[:, :, o].reshape(4 * N, HT),
            CONTRACT_FIRST, preferred_element_type=F32,
        )


    @pl.loop(0, H // HT)
    def _(j):
        o = pl.ds(pl.multiple_of(j * HT, HT), HT)
        gp[o, :] = lax.dot_general(
            act[:, :, o].reshape(4 * N, HT), cs[...].reshape(4 * N, DC),
            CONTRACT_FIRST, preferred_element_type=F32,
        )


    for c in c_fa:
        c.wait_recv()
    for q in range(4):
        n = min(16, KS * KS - 16 * q)
        for t in range(S):
            gf_ref[pl.ds(16 * q, n), pl.ds(t * CH, CH)] = fall[q, t].astype(F32)[:n]
    for c in c_bo + c_gi:
        c.wait_recv()
    for c in [c_cot, c_nrm] + c_pn + c_po + c_core + c_st + c_bo + c_f + c_fz + c_gi + c_fa:
        c.wait_send()
    for c in (to_hi, gto_hi):
        @pl.when(has_hi)
        def _():
            c.wait_send()
    for c in (to_lo, gto_lo):
        @pl.when(has_lo)
        def _():
            c.wait_send()


def store_kernel(*refs):
    sems = refs[-1]
    half = (len(refs) - 1) // 2
    copies = [
        pltpu.make_async_copy(refs[i], refs[half + i], sems.at[i]) for i in range(half)
    ]
    for c in copies:
        c.start()
    for c in copies:
        c.wait()


def kernel_body(maps_in, filters, w_expand, w_project, cotangent):
    R, W, C = maps_in.shape
    H = w_expand.shape[1]
    S = lax.axis_size("shard")
    N, CH, DC, RE = R * W, C // S, C // 4, R + 2 * REACH
    VM = pltpu.VMEM
    scratch = [
        VM((R, W, C), BF16), VM((KS * KS, C), BF16), VM((N, C), BF16),
        VM((C, H), BF16), VM((H, C), BF16), VM((56, C), F32),
        VM((RE, W + 2 * PAD, C), F32),
        VM((REACH, W, C), BF16), VM((REACH, W, C), BF16),
        VM((N, C), F32), VM((N, C), F32), VM((N, LANE), F32), VM((N, H), F32),
        VM((2, N, C), BF16), VM((N, C), BF16),
        VM((4, N, H), BF16), VM((4, N, H), BF16),
        VM((4, N, DC), BF16), VM((4, N, DC), BF16),
        VM((S, N, CH), BF16), VM((S, N, CH), BF16),
        VM((S, N, CH), BF16), VM((S, N, CH), BF16),
        VM((8, N), F32), VM((S, 8, N), F32),
        VM((N, CH), BF16), VM((REACH * W, CH), BF16), VM((REACH * W, CH), BF16),
        VM((RE, W + 2 * PAD, CH), F32),
        VM((64, CH), F32), VM((64, CH), BF16), VM((4, 16, CH), BF16), VM((4, S, 16, CH), BF16),
        pltpu.SemaphoreType.DMA((48,)), pltpu.SemaphoreType.DMA((48,)),
        pltpu.SemaphoreType.DMA((8,)),
    ]
    vmem = pl.BlockSpec(memory_space=pltpu.VMEM)
    anys = pl.BlockSpec(memory_space=pl.ANY)
    shapes = (
        jax.ShapeDtypeStruct((N, C), BF16),
        jax.ShapeDtypeStruct((N, C), BF16),
        jax.ShapeDtypeStruct((DC, H), F32),
        jax.ShapeDtypeStruct((H, DC), F32),
        jax.ShapeDtypeStruct((KS * KS, C), F32),
    )
    results = pl.pallas_call(
        functools.partial(kernel, S, R, W, C, H),
        out_shape=shapes,
        in_specs=[pl.BlockSpec(memory_space=pltpu.HBM)] * 5,
        out_specs=(vmem,) * 5,
        scratch_shapes=scratch,
        compiler_params=pltpu.CompilerParams(
            collective_id=0, has_side_effects=True, vmem_limit_bytes=44 * 1024 * 1024
        ),
    )(maps_in, filters, cotangent.reshape(N, C), w_expand, w_project)
    out, gin, ge, gp, gf = pl.pallas_call(
        store_kernel,
        out_shape=shapes,
        in_specs=[anys] * 5,
        out_specs=(anys,) * 5,
        scratch_shapes=[pltpu.SemaphoreType.DMA((5,))],
        compiler_params=pltpu.CompilerParams(vmem_limit_bytes=1024 * 1024),
    )(*results)
    return (out.reshape(R, W, C), gin.reshape(R, W, C), ge, gp, gf)


def body(maps_in, filters, w_expand, w_project, cotangent):
    rows, cols, width = maps_in.shape
    hid = w_expand.shape[1]
    shards = lax.axis_size("shard")
    fits = (
        lax.axis_size("dp") == 4
        and width % (shards * LANE) == 0
        and width % (4 * LANE) == 0
        and hid % LANE == 0
        and shards > 1
        and rows >= REACH
        and rows * cols == LANE
        and cols % 16 == 0
    )
    run = kernel_body if fits else plain_body
    return run(maps_in, filters, w_expand, w_project, cotangent)


def solution(mesh):
    placed = (
        P(("groups", "dp"), None, None),
        P(),
        P(None, "shard"),
        P("shard", None),
        P(("groups", "dp"), None, None),
    )
    return jax.shard_map(
        body,
        mesh=mesh,
        in_specs=placed,
        out_specs=(
            P(("groups", "dp"), None, None),
            P(("groups", "dp"), None, None),
            P(("groups", "dp"), "shard"),
            P(("groups", "shard"), "dp"),
            P("groups", None),
        ),
        check_vma=False,
    )
```

```python
import functools

import jax
import jax.numpy as jnp
from jax import lax
from jax.experimental import pallas as pl
from jax.experimental.pallas import tpu as pltpu
from jax.sharding import PartitionSpec as P

KS = 7
REACH = KS // 2
LANE = 128
PAD = 8
F32 = jnp.float32
BF16 = jnp.bfloat16
MESH = pl.DeviceIdType.MESH


def extended(block, sides, width):
    for axis, dim in sides:
        count = lax.axis_size(axis)
        forward = [(i, i + 1) for i in range(count - 1)]
        backward = [(target, source) for source, target in forward]
        low = lax.ppermute(
            lax.slice_in_dim(block, block.shape[dim] - width, None, axis=dim), axis, forward
        )
        high = lax.ppermute(lax.slice_in_dim(block, 0, width, axis=dim), axis, backward)
        block = jnp.concatenate([low, block, high], axis=dim)
    return block


def gelu_parts(hidden):
    cdf = 0.5 * (1.0 + lax.erf(hidden * 0.7071067811865476))
    density = jnp.exp(-0.5 * hidden * hidden) * 0.3989422804014327
    return (hidden * cdf, cdf + hidden * density)


def norm_stats(conv_rows):
    centered = conv_rows - jnp.mean(conv_rows, axis=-1, keepdims=True)
    variance = jnp.mean(centered * centered, axis=-1, keepdims=True)
    inv_scale = lax.rsqrt(variance + 1e-06)
    return (centered * inv_scale, inv_scale)


def norm_back(d_normed, scaled, inv_scale):
    first = jnp.mean(d_normed, axis=-1, keepdims=True)
    second = jnp.mean(d_normed * scaled, axis=-1, keepdims=True)
    return inv_scale * (d_normed - first - scaled * second)


def plain_body(maps_in, filters, w_expand, w_project, cotangent):
    reach = KS // 2
    rows, cols, width = maps_in.shape
    count = rows * cols
    taps_f32 = filters.astype(jnp.float32)
    halo_in = extended(maps_in, (("dp", 0),), reach)
    padded_in = jnp.pad(halo_in, ((0, 0), (reach, reach), (0, 0)))
    conv_out = jnp.zeros((rows, cols, width), jnp.float32)
    for tap in range(KS * KS):
        tap_row, tap_col = divmod(tap, KS)
        conv_out = (
            conv_out
            + padded_in[tap_row : tap_row + rows, tap_col : tap_col + cols].astype(jnp.float32)
            * taps_f32[tap]
        )
    scaled, inv_scale = norm_stats(conv_out.reshape(count, width))
    normed = scaled.astype(jnp.bfloat16)
    hidden = jnp.dot(normed, w_expand, preferred_element_type=jnp.float32)
    activ, slope = gelu_parts(hidden)
    act = activ.astype(jnp.bfloat16)
    partial_out = jnp.dot(act, w_project, preferred_element_type=jnp.float32)
    cot_rows = cotangent.reshape(count, width)
    summed_out = lax.psum(partial_out.astype(jnp.bfloat16), "shard").astype(jnp.float32)
    d_act = lax.dot_general(
        cot_rows, w_project, (((1,), (1,)), ((), ())), preferred_element_type=jnp.float32
    )
    d_hidden = (d_act * slope).astype(jnp.bfloat16)
    grad_proj_local = lax.dot_general(
        act, cot_rows, (((0,), (0,)), ((), ())), preferred_element_type=jnp.float32
    )
    grad_exp_local = lax.dot_general(
        normed, d_hidden, (((0,), (0,)), ((), ())), preferred_element_type=jnp.float32
    )
    partial_norm = lax.dot_general(
        d_hidden, w_expand, (((1,), (1,)), ((), ())), preferred_element_type=jnp.float32
    )
    d_normed = lax.psum(partial_norm.astype(jnp.bfloat16), "shard").astype(jnp.float32)
    d_conv = norm_back(d_normed, scaled, inv_scale).astype(jnp.bfloat16)
    block_out = (
        (maps_in.reshape(count, width).astype(jnp.float32) + summed_out)
        .astype(jnp.bfloat16)
        .reshape(rows, cols, width)
    )
    grad_expand, grad_project = (
        lax.psum_scatter(
            grad_exp_local.astype(jnp.bfloat16), "dp", scatter_dimension=0, tiled=True
        ).astype(jnp.float32),
        lax.psum_scatter(
            grad_proj_local.astype(jnp.bfloat16), "dp", scatter_dimension=1, tiled=True
        ).astype(jnp.float32),
    )
    d_conv = d_conv.reshape(rows, cols, width)
    halo_grad = extended(d_conv, (("dp", 0),), reach)
    padded_grad = jnp.pad(halo_grad, ((0, 0), (reach, reach), (0, 0)))
    conv_grad = d_conv.astype(jnp.float32)
    back_sum = cotangent.astype(jnp.float32)
    filter_rows = []
    for tap in range(KS * KS):
        tap_row, tap_col = divmod(tap, KS)
        back_sum = (
            back_sum
            + padded_grad[
                2 * reach - tap_row : 2 * reach - tap_row + rows,
                2 * reach - tap_col : 2 * reach - tap_col + cols,
            ].astype(jnp.float32)
            * taps_f32[tap]
        )
        filter_rows.append(
            jnp.sum(
                conv_grad
                * padded_in[tap_row : tap_row + rows, tap_col : tap_col + cols].astype(jnp.float32),
                axis=(0, 1),
            )
        )
    grad_input = back_sum.astype(jnp.bfloat16)
    grad_filters = lax.psum(jnp.stack(filter_rows, axis=0).astype(jnp.bfloat16), "dp").astype(
        jnp.float32
    )
    return (block_out, grad_input, grad_expand, grad_project, grad_filters)


CONTRACT_LAST = (((1,), (1,)), ((), ()))
CONTRACT_FIRST = (((0,), (0,)), ((), ()))


def kernel(
    S, R, W, C, H,
    maps_hbm, fil_hbm, cot_hbm, we_hbm, wp_hbm,
    out_ref, gin_ref, ge, gp, gf_ref,
    maps_ref, fil_ref, cot_ref, we, wp, fil, mp, halo_lo, halo_hi, conv, scaled, invs, dact,
    nrm, cots, act, dh, ns, cs, pn, rn, po, ro, st, rst,
    dcv, dlo, dhi, dpad, fpart, fsend, fsum, fall,
    send, recv, loc,
):
    N = R * W
    CH = C // S
    DC = C // 4
    g = lax.axis_index("groups")
    s = lax.axis_index("shard")
    d = lax.axis_index("dp")
    pair_core = d + 1 - 2 * lax.rem(d, 2)
    pair_chip = lax.rem(d + 2, 4)
    peers = [lax.rem(s + k, S) for k in range(S)]
    has_lo = d > 0
    has_hi = d < 3

    def chan(i):
        return pl.ds(pl.multiple_of(i * CH, LANE), CH)

    def dpcols(i):
        return pl.ds(pl.multiple_of(i * DC, LANE), DC)

    counter = [0]

    def remote(src, dst, shard, dp):
        i = counter[0]
        counter[0] += 1
        return pltpu.make_async_remote_copy(
            src_ref=src, dst_ref=dst, send_sem=send.at[i], recv_sem=recv.at[i],
            device_id=(g, shard, dp), device_id_type=MESH,
        )

    def move(src, dst, i):
        return pltpu.make_async_copy(src, dst, loc.at[i])

    cp_wp = move(wp_hbm, wp, 0)
    cp_we = move(we_hbm, we, 1)
    cp_maps = move(maps_hbm, maps_ref, 2)
    cp_fil = move(fil_hbm, fil_ref, 3)
    cp_cot = move(cot_hbm, cot_ref, 4)
    cp_maps.start()
    cp_cot.start()
    cp_fil.start()
    cp_wp.start()
    cp_we.start()

    barrier = pltpu.get_barrier_semaphore()
    for k in range(1, S):
        pl.semaphore_signal(barrier, inc=1, device_id=(g, peers[k], d), device_id_type=MESH)
    for k in range(1, 4):
        pl.semaphore_signal(
            barrier, inc=1, device_id=(g, s, lax.rem(d + k, 4)), device_id_type=MESH
        )
    pl.semaphore_wait(barrier, S - 1 + 3)

    lo_dp = jnp.maximum(d - 1, 0)
    hi_dp = jnp.minimum(d + 1, 3)
    to_hi = remote(maps_hbm.at[pl.ds(R - REACH, REACH)], halo_lo, s, hi_dp)
    to_lo = remote(maps_hbm.at[pl.ds(0, REACH)], halo_hi, s, lo_dp)

    @pl.when(has_hi)
    def _():
        to_hi.start()

    @pl.when(has_lo)
    def _():
        to_lo.start()

    cp_maps.wait()
    cp_fil.wait()
    fil[pl.ds(0, KS * KS), :] = fil_ref[...].astype(F32)
    for r in range(R + 2 * REACH):
        mp[r, pl.ds(0, PAD), :] = jnp.zeros((PAD, C), F32)
        mp[r, pl.ds(PAD + W, PAD), :] = jnp.zeros((PAD, C), F32)
        dpad[r, pl.ds(0, PAD), :] = jnp.zeros((PAD, CH), F32)
        dpad[r, pl.ds(PAD + W, PAD), :] = jnp.zeros((PAD, CH), F32)
    for r in range(R):
        mp[REACH + r, pl.ds(PAD, W), :] = maps_ref[r].astype(F32)

    HT = 256 if H % 256 == 0 else LANE
    cp_cot.wait()
    cp_wp.wait()

    @pl.loop(0, H // HT)
    def _(j):
        o = pl.multiple_of(j * HT, HT)
        dact[:, pl.ds(o, HT)] = lax.dot_general(
            cot_ref[...], wp[pl.ds(o, HT), :], CONTRACT_LAST, preferred_element_type=F32
        )

    def fill(cond, copy, buf, target, base, width):
        @pl.when(cond)
        def _():
            copy.wait_recv()
            for r in range(REACH):
                if len(buf.shape) == 3:
                    target[base + r, pl.ds(PAD, W), :] = buf[r].astype(F32)
                else:
                    target[base + r, pl.ds(PAD, W), :] = buf[pl.ds(r * W, W), :].astype(F32)

        @pl.when(jnp.logical_not(cond))
        def _():
            for r in range(REACH):
                target[base + r, pl.ds(PAD, W), :] = jnp.zeros((W, width), F32)

    fill(has_lo, to_hi, halo_lo, mp, 0, C)
    fill(has_hi, to_lo, halo_hi, mp, REACH + R, C)
    c_cot = remote(cot_hbm, cots, s, pair_chip)
    c_cot.start()

    @pl.loop(0, C // LANE)
    def _(t):
        o = pl.ds(pl.multiple_of(t * LANE, LANE), LANE)
        accs = [jnp.zeros((W, LANE), F32) for _ in range(R)]
        for b in range(KS):
            taps = [fil[pl.ds(a * KS + b, 1), o] for a in range(KS)]
            for rin in range(R + 2 * REACH):
                v = mp[rin, pl.ds(PAD - REACH + b, W), o]
                for r in range(R):
                    if 0 <= rin - r < KS:
                        accs[r] = accs[r] + v * taps[rin - r]
        for r in range(R):
            conv[pl.ds(r * W, W), o] = accs[r]

    @pl.loop(0, N // 16)
    def _(t):
        o = pl.ds(pl.multiple_of(t * 16, 16), 16)
        sc, inv = norm_stats(conv[o, :])
        scaled[o, :] = sc
        invs[o, :] = jnp.broadcast_to(inv, (16, LANE))
        nrm[0, o, :] = sc.astype(BF16)

    c_nrm = remote(nrm.at[0], nrm.at[1], s, pair_chip)
    c_nrm.start()

    cp_we.wait()

    @pl.loop(0, H // HT)
    def _(j):
        o = pl.ds(pl.multiple_of(j * HT, HT), HT)
        hid = jnp.dot(nrm[0], we[:, o], preferred_element_type=F32)
        a, slope = gelu_parts(hid)
        act[0, :, o] = a.astype(BF16)
        dh[0, :, o] = (dact[:, o] * slope).astype(BF16)

    c_pn = []
    for k in list(range(1, S)) + [0]:
        t = peers[k]
        pn[k] = lax.dot_general(
            dh[0], we[chan(t), :], CONTRACT_LAST, preferred_element_type=F32
        ).astype(BF16)
        if k:
            c = remote(pn.at[k], rn.at[k], t, d)
            c.start()
            c_pn.append(c)
    c_po = []
    for k in list(range(1, S)) + [0]:
        t = peers[k]
        po[k] = jnp.dot(act[0], wp[:, chan(t)], preferred_element_type=F32).astype(BF16)
        if k:
            c_po.append(remote(po.at[k], ro.at[k], t, d))

    own = chan(s)
    for c in c_pn:
        c.wait_recv()
    dn = pn[0].astype(F32)
    for k in range(1, S):
        dn = dn + rn[k].astype(F32)
    sc = scaled[:, own]
    first = jnp.sum(dn, axis=-1, keepdims=True)
    second = jnp.sum(dn * sc, axis=-1, keepdims=True)
    lane = lax.broadcasted_iota(jnp.int32, (N, LANE), 1)
    st[...] = jnp.where(lane == 0, first, jnp.where(lane == 1, second, 0.0)).T[:8]
    c_st = []
    for k in range(1, S):
        c = remote(st, rst.at[k], peers[k], d)
        c.start()
        c_st.append(c)
    conv[:, pl.ds(0, CH)] = dn

    for c in c_po:
        c.start()

    for c in c_st:
        c.wait_recv()
    tot = st[...]
    for k in range(1, S):
        tot = tot + rst[k]
    tot = jnp.concatenate([tot, jnp.zeros((LANE - 8, N), F32)], axis=0).T * (1.0 / C)
    dcv[...] = (
        invs[:, pl.ds(0, 1)]
        * (conv[:, pl.ds(0, CH)] - tot[:, 0:1] - scaled[:, own] * tot[:, 1:2])
    ).astype(BF16)
    gto_hi = remote(dcv.at[pl.ds((R - REACH) * W, REACH * W)], dlo, s, hi_dp)
    gto_lo = remote(dcv.at[pl.ds(0, REACH * W)], dhi, s, lo_dp)

    @pl.when(has_hi)
    def _():
        gto_hi.start()

    @pl.when(has_lo)
    def _():
        gto_lo.start()

    for r in range(R):
        dpad[REACH + r, pl.ds(PAD, W), :] = dcv[pl.ds(r * W, W), :].astype(F32)

    fpart[...] = jnp.zeros_like(fpart)

    @pl.loop(0, CH // LANE)
    def _(t):
        o = pl.ds(pl.multiple_of(t * LANE, LANE), LANE)
        so = pl.ds(pl.multiple_of(s * CH + t * LANE, LANE), LANE)
        grads = [dpad[REACH + r, pl.ds(PAD, W), o] for r in range(R)]
        for b in range(KS):
            sums = [jnp.zeros((W, LANE), F32) for _ in range(KS)]
            for rin in range(R + 2 * REACH):
                v = mp[rin, pl.ds(PAD - REACH + b, W), so]
                for r in range(R):
                    if 0 <= rin - r < KS:
                        sums[rin - r] = sums[rin - r] + v * grads[r]
            for a in range(KS):
                fpart[pl.ds(a * KS + b, 1), o] = jnp.sum(sums[a], axis=0, keepdims=True)

    fsend[...] = fpart[...].astype(BF16)
    fsum[d] = fsend[pl.ds(pl.multiple_of(d * 16, 16), 16), :]
    c_f = []
    for k in range(1, 4):
        t = lax.rem(d + k, 4)
        c = remote(
            fsend.at[pl.ds(pl.multiple_of(t * 16, 16), 16)], fsum.at[d], s, t
        )
        c.start()
        c_f.append(c)

    fill(has_lo, gto_hi, dlo, dpad, 0, CH)
    fill(has_hi, gto_lo, dhi, dpad, REACH + R, CH)

    @pl.loop(0, CH // LANE)
    def _(t):
        o = pl.ds(pl.multiple_of(t * LANE, LANE), LANE)
        so = pl.ds(pl.multiple_of(s * CH + t * LANE, LANE), LANE)
        accs = [cot_ref[pl.ds(r * W, W), so].astype(F32) for r in range(R)]
        for b in range(KS):
            taps = [fil[pl.ds(a * KS + b, 1), so] for a in range(KS)]
            for rin in range(R + 2 * REACH):
                v = dpad[rin, pl.ds(PAD + REACH - b, W), o]
                for r in range(R):
                    a = r + 2 * REACH - rin
                    if 0 <= a < KS:
                        accs[r] = accs[r] + v * taps[a]
        for r in range(R):
            gin_ref[pl.ds(r * W, W), so] = accs[r].astype(BF16)

    c_gi = []
    for k in range(1, S):
        c = remote(gin_ref.at[:, own], gin_ref.at[:, own], peers[k], d)
        c.start()
        c_gi.append(c)

    for c in c_f:
        c.wait_recv()
    fa = (fsum[0].astype(F32) + fsum[1].astype(F32)) + (
        fsum[2].astype(F32) + fsum[3].astype(F32)
    )
    fall[d, s] = fa.astype(BF16)
    c_fz = []
    for k in range(1, S):
        c = remote(fall.at[d, s], fall.at[d, s], peers[k], d)
        c.start()
        c_fz.append(c)

    for c in c_po:
        c.wait_recv()
    for r in range(R):
        rows = pl.ds(r * W, W)
        total = po[0, rows, :].astype(F32)
        for k in range(1, S):
            total = total + ro[k, rows, :].astype(F32)
        out_ref[rows, own] = (mp[REACH + r, pl.ds(PAD, W), own] + total).astype(BF16)
    c_bo = []
    for k in range(1, S):
        c = remote(out_ref.at[:, own], out_ref.at[:, own], peers[k], d)
        c.start()
        c_bo.append(c)

    c_cot.wait_recv()
    c_nrm.wait_recv()

    @pl.loop(0, H // HT)
    def _(j):
        o = pl.ds(pl.multiple_of(j * HT, HT), HT)
        hid = jnp.dot(nrm[1], we[:, o], preferred_element_type=F32)
        a, slope = gelu_parts(hid)
        act[1, :, o] = a.astype(BF16)
        da = lax.dot_general(
            cots[...], wp[o, :], CONTRACT_LAST, preferred_element_type=F32
        )
        dh[1, :, o] = (da * slope).astype(BF16)

    pc = dpcols(pair_core)
    mine = dpcols(d)
    c_core = [
        remote(act.at[pl.ds(0, 2)], act.at[pl.ds(2, 2)], s, pair_core),
        remote(dh.at[pl.ds(0, 2)], dh.at[pl.ds(2, 2)], s, pair_core),
        remote(nrm.at[pl.ds(0, 2), :, pc], ns.at[pl.ds(2, 2)], s, pair_core),
        remote(cot_ref.at[:, pc], cs.at[2], s, pair_core),
        remote(cots.at[:, pc], cs.at[3], s, pair_core),
    ]
    for c in c_core:
        c.start()
    ns[0] = nrm[0, :, mine]
    ns[1] = nrm[1, :, mine]
    cs[0] = cot_ref[:, mine]
    cs[1] = cots[:, mine]

    for c in c_fz:
        c.wait_recv()
    c_fa = []
    for k in range(1, 4):
        c = remote(fall.at[d], fall.at[d], s, lax.rem(d + k, 4))
        c.start()
        c_fa.append(c)

    for c in c_core:
        c.wait_recv()

    @pl.loop(0, H // HT)
    def _(j):
        o = pl.ds(pl.multiple_of(j * HT, HT), HT)
        ge[:, o] = lax.dot_general(
            ns[...].reshape(4 * N, DC), dh[:, :, o].reshape(4 * N, HT),
            CONTRACT_FIRST, preferred_element_type=F32,
        )


    @pl.loop(0, H // HT)
    def _(j):
        o = pl.ds(pl.multiple_of(j * HT, HT), HT)
        gp[o, :] = lax.dot_general(
            act[:, :, o].reshape(4 * N, HT), cs[...].reshape(4 * N, DC),
            CONTRACT_FIRST, preferred_element_type=F32,
        )


    for c in c_fa:
        c.wait_recv()
    for q in range(4):
        n = min(16, KS * KS - 16 * q)
        for t in range(S):
            gf_ref[pl.ds(16 * q, n), pl.ds(t * CH, CH)] = fall[q, t].astype(F32)[:n]
    for c in c_bo + c_gi:
        c.wait_recv()
    for c in [c_cot, c_nrm] + c_pn + c_po + c_core + c_st + c_bo + c_f + c_fz + c_gi + c_fa:
        c.wait_send()
    for c in (to_hi, gto_hi):
        @pl.when(has_hi)
        def _():
            c.wait_send()
    for c in (to_lo, gto_lo):
        @pl.when(has_lo)
        def _():
            c.wait_send()


def store_kernel(*refs):
    sems = refs[-1]
    half = (len(refs) - 1) // 2
    copies = [
        pltpu.make_async_copy(refs[i], refs[half + i], sems.at[i]) for i in range(half)
    ]
    for c in copies:
        c.start()
    for c in copies:
        c.wait()


def kernel_body(maps_in, filters, w_expand, w_project, cotangent):
    R, W, C = maps_in.shape
    H = w_expand.shape[1]
    S = lax.axis_size("shard")
    N, CH, DC, RE = R * W, C // S, C // 4, R + 2 * REACH
    VM = pltpu.VMEM
    scratch = [
        VM((R, W, C), BF16), VM((KS * KS, C), BF16), VM((N, C), BF16),
        VM((C, H), BF16), VM((H, C), BF16), VM((56, C), F32),
        VM((RE, W + 2 * PAD, C), F32),
        VM((REACH, W, C), BF16), VM((REACH, W, C), BF16),
        VM((N, C), F32), VM((N, C), F32), VM((N, LANE), F32), VM((N, H), F32),
        VM((2, N, C), BF16), VM((N, C), BF16),
        VM((4, N, H), BF16), VM((4, N, H), BF16),
        VM((4, N, DC), BF16), VM((4, N, DC), BF16),
        VM((S, N, CH), BF16), VM((S, N, CH), BF16),
        VM((S, N, CH), BF16), VM((S, N, CH), BF16),
        VM((8, N), F32), VM((S, 8, N), F32),
        VM((N, CH), BF16), VM((REACH * W, CH), BF16), VM((REACH * W, CH), BF16),
        VM((RE, W + 2 * PAD, CH), F32),
        VM((64, CH), F32), VM((64, CH), BF16), VM((4, 16, CH), BF16), VM((4, S, 16, CH), BF16),
        pltpu.SemaphoreType.DMA((48,)), pltpu.SemaphoreType.DMA((48,)),
        pltpu.SemaphoreType.DMA((8,)),
    ]
    vmem = pl.BlockSpec(memory_space=pltpu.VMEM)
    anys = pl.BlockSpec(memory_space=pl.ANY)
    shapes = (
        jax.ShapeDtypeStruct((N, C), BF16),
        jax.ShapeDtypeStruct((N, C), BF16),
        jax.ShapeDtypeStruct((DC, H), F32),
        jax.ShapeDtypeStruct((H, DC), F32),
        jax.ShapeDtypeStruct((KS * KS, C), F32),
    )
    results = pl.pallas_call(
        functools.partial(kernel, S, R, W, C, H),
        out_shape=shapes,
        in_specs=[pl.BlockSpec(memory_space=pltpu.HBM)] * 5,
        out_specs=(vmem,) * 5,
        scratch_shapes=scratch,
        compiler_params=pltpu.CompilerParams(
            collective_id=0, has_side_effects=True, vmem_limit_bytes=44 * 1024 * 1024
        ),
    )(maps_in, filters, cotangent.reshape(N, C), w_expand, w_project)
    out, gin, ge, gp, gf = pl.pallas_call(
        store_kernel,
        out_shape=shapes,
        in_specs=[anys] * 5,
        out_specs=(anys,) * 5,
        scratch_shapes=[pltpu.SemaphoreType.DMA((5,))],
        compiler_params=pltpu.CompilerParams(vmem_limit_bytes=1024 * 1024),
    )(*results)
    return (out.reshape(R, W, C), gin.reshape(R, W, C), ge, gp, gf)


def body(maps_in, filters, w_expand, w_project, cotangent):
    rows, cols, width = maps_in.shape
    hid = w_expand.shape[1]
    shards = lax.axis_size("shard")
    fits = (
        lax.axis_size("dp") == 4
        and width % (shards * LANE) == 0
        and width % (4 * LANE) == 0
        and hid % LANE == 0
        and shards > 1
        and rows >= REACH
        and rows * cols == LANE
        and cols % 16 == 0
    )
    run = kernel_body if fits else plain_body
    return run(maps_in, filters, w_expand, w_project, cotangent)


def solution(mesh):
    placed = (
        P(("groups", "dp"), None, None),
        P(),
        P(None, "shard"),
        P("shard", None),
        P(("groups", "dp"), None, None),
    )
    return jax.shard_map(
        body,
        mesh=mesh,
        in_specs=placed,
        out_specs=(
            P(("groups", "dp"), None, None),
            P(("groups", "dp"), None, None),
            P(("groups", "dp"), "shard"),
            P(("groups", "shard"), "dp"),
            P("groups", None),
        ),
        check_vma=False,
    )
```
